32 devices in a mesh: dp: 4 (over y, core), seq: 8 (over z, x).
Axes of the slice: x: 2, y: 2, z: 4, core: 2. Of those that a mesh axis runs over, the one named last changes fastest.
Arguments:
- queries: bfloat16 [4, 1024, 1152], P('dp', 'seq'), may hold values from -12 to 12
- keys: bfloat16 [4, 1024, 1152], P('dp', 'seq'), may hold values from -12 to 12
- values: bfloat16 [4, 1024, 1152], P('dp', 'seq'), may hold values from -6 to 6
- out_weight: bfloat16 [1152, 1152], replicated, may hold values from -0.1875 to 0.1875
- out_grad: bfloat16 [4, 1024, 1152], P('dp', 'seq'), may hold values from -48 to 48
- lengths: int32 [4, 4], P('dp'), may hold values from 128 to 384, as said below
Outputs:
- query_grad: float32 [4, 1024, 1152], P('dp', 'seq')
- key_grad: float32 [4, 1024, 1152], P('dp', 'seq')
- value_grad: float32 [4, 1024, 1152], P('dp', 'seq')
- weight_grad: float32 [1152, 1152], P('seq')
The draws below stay inside these ranges and needn't reach their ends.
Inputs may be any that keep to these rules, and one draw needn't show every extreme that they name: Each row's 4 lengths sum to 1024; the largest in each row is exactly 384.
All inputs are finite; a program needn't handle non-finite values.
Results may differ from the reference program's by a relative error of at most 0.012.
The reference program's roundings to bfloat16 on the way count: a program that leaves them out, or rounds other values in their place, can miss the bound.
Values may be sent and summed in bfloat16 or wider, within the bound.
No kernel may reach another device: no remote copies, remote signals or barrier semaphores. Data moves between devices by JAX's collectives and lax.ppermute only.
A program may use at most 128 MiB of HBM per device.

```python
import jax
import jax.numpy as jnp
from jax import lax

D = 1152
HEADS = 16
HEAD_DIM = 72
TOK_DEV = 128
MAXLEN = 384
BATCH = 4
TOKENS = 1024
NIMG = 4
REACH = 3
ALL_TOK = 4096


def draw_queries(key, part):
    drawn = jnp.clip(jax.random.normal(jax.random.fold_in(key, 1), (BATCH, TOKENS, D), jnp.float32), -6.0, 6.0)
    return jnp.clip(drawn, -12.0, 12.0).astype(jnp.bfloat16)


def draw_keys(key, part):
    drawn = jnp.clip(jax.random.normal(jax.random.fold_in(key, 2), (BATCH, TOKENS, D), jnp.float32), -6.0, 6.0)
    return jnp.clip(drawn, -12.0, 12.0).astype(jnp.bfloat16)


def draw_lengths(key, part):
    least = MAXLEN // 3
    ceiling = MAXLEN - least
    count = NIMG - 1
    extra = TOKENS - MAXLEN - count * least
    share = extra // count
    remain = extra - share * count
    spread = max(min(share, ceiling - share), 1)
    pairs = count // 2

    def one_row(row):
        row_key = jax.random.fold_in(key, row)
        order_perm = jax.random.permutation(jax.random.fold_in(row_key, 1), count).astype(jnp.int32)
        amount = jax.random.randint(jax.random.fold_in(row_key, 2), (pairs,), 0, spread, dtype=jnp.int32)
        amount = amount.at[0].set(share)
        delta = jnp.zeros((count,), jnp.int32)
        delta = delta.at[order_perm[0:2 * pairs:2]].add(amount)
        delta = delta.at[order_perm[1:2 * pairs:2]].add(-amount)
        bump_order = jnp.concatenate([order_perm[0:1], order_perm[2:], order_perm[1:2]])
        bumps = (jnp.arange(count, dtype=jnp.int32) < remain).astype(jnp.int32)
        delta = delta.at[bump_order].add(bumps)
        others = least + share + delta
        place = jax.random.randint(jax.random.fold_in(row_key, 3), (), 0, NIMG, dtype=jnp.int32)
        slots = jnp.arange(NIMG, dtype=jnp.int32)
        source = jnp.clip(jnp.where(slots < place, slots, slots - 1), 0, count - 1)
        return jnp.where(slots == place, MAXLEN, others[source]).astype(jnp.int32)
    return lax.map(one_row, jnp.arange(BATCH, dtype=jnp.int32))


def levels(stream_key, dims, pieces, low, largest):
    def one(position, shards_of):
        draws = jax.random.uniform(jax.random.fold_in(jax.random.fold_in(stream_key, 6), position), (shards_of,), jnp.float32, low / len(pieces), largest / len(pieces))
        return jnp.repeat(jnp.exp(draws), dims[position] // shards_of).reshape((-1,) + (1,) * (len(dims) - position - 1))

    gain = one(*pieces[0])
    for cut in pieces[1:]:
        gain = gain * one(*cut)
    return gain


def bell_draw(key, dims, width, limit, split=(), kind=jnp.bfloat16):
    values = jax.random.normal(key, dims, jnp.float32) * width
    if len(split) > 0:
        values = levels(key, dims, split, -0.22, 0.18) * values
    return jnp.clip(values, min=-limit, max=limit).astype(kind)


def setup_inputs(seed: int = 0) -> dict:
    key_list = jax.random.split(jax.random.key(seed), 7)
    queries = draw_queries(jax.random.fold_in(key_list[6], 71), 0)
    keys = draw_keys(jax.random.fold_in(key_list[6], 71), 0)
    values = bell_draw(key_list[2], (BATCH, TOKENS, D), 1.0, 6.0, ((0, 4), (1, 8)))
    out_weight = bell_draw(key_list[3], (D, D), D ** -0.5, 0.1875)
    out_grad = bell_draw(key_list[4], (BATCH, TOKENS, D), 8.0, 48.0, ((0, 4), (1, 8)))
    lengths = draw_lengths(jax.random.fold_in(key_list[6], 71), 0)
    return dict(queries=queries, keys=keys, values=values, out_weight=out_weight, out_grad=out_grad, lengths=lengths)


def reference(queries, keys, values, out_weight, out_grad, lengths):
    score_scale = HEAD_DIM ** -0.5
    pad_rows = REACH * TOK_DEV
    window = (2 * REACH + 1) * TOK_DEV

    def one_group(inputs):
        q_all, k_all, v_all, dy_all, lens_row = inputs
        image_ends = jnp.cumsum(lens_row).astype(jnp.int32)
        positions = jnp.arange(TOKENS, dtype=jnp.int32)
        image_ids = jnp.sum((positions[:, None] >= image_ends[None, :]).astype(jnp.int32), axis=1).astype(jnp.int32)
        keys_pad = jnp.pad(k_all, ((pad_rows, pad_rows), (0, 0)))
        values_pad = jnp.pad(v_all, ((pad_rows, pad_rows), (0, 0)))
        ids_pad = jnp.pad(image_ids, (pad_rows, pad_rows), constant_values=-1).astype(jnp.int32)
        d_all = jnp.dot(dy_all, out_weight.T, preferred_element_type=jnp.float32).astype(jnp.bfloat16)

        def block_step(carried, block):
            k_grads, v_grads, w_grad = carried
            start = (block * TOK_DEV).astype(jnp.int32)
            q_blk = lax.dynamic_slice_in_dim(q_all, start, TOK_DEV, 0)
            d_blk = lax.dynamic_slice_in_dim(d_all, start, TOK_DEV, 0)
            dy_blk = lax.dynamic_slice_in_dim(dy_all, start, TOK_DEV, 0)
            q_ids = lax.dynamic_slice_in_dim(image_ids, start, TOK_DEV, 0)
            k_win = lax.dynamic_slice_in_dim(keys_pad, start, window, 0)
            v_win = lax.dynamic_slice_in_dim(values_pad, start, window, 0)
            k_ids = lax.dynamic_slice_in_dim(ids_pad, start, window, 0)
            q_heads = q_blk.astype(jnp.float32).reshape(TOK_DEV, HEADS, HEAD_DIM)
            k_heads = k_win.astype(jnp.float32).reshape(window, HEADS, HEAD_DIM)
            v_heads = v_win.astype(jnp.float32).reshape(window, HEADS, HEAD_DIM)
            d_heads = d_blk.astype(jnp.float32).reshape(TOK_DEV, HEADS, HEAD_DIM)
            scores = jnp.einsum('qhd,khd->hqk', q_heads, k_heads) * score_scale
            same_image = q_ids[:, None] == k_ids[None, :]
            scores = jnp.where(same_image[None, :, :], scores, -1.0e30)
            row_max = jnp.max(scores, axis=2)
            log_norm = row_max + jnp.log(jnp.sum(jnp.exp(scores - row_max[:, :, None]), axis=2))
            weights = jnp.exp(scores - log_norm[:, :, None]).astype(jnp.bfloat16)
            weights_f = weights.astype(jnp.float32)
            attended = jnp.einsum('hqk,khd->qhd', weights_f, v_heads).reshape(TOK_DEV, D).astype(jnp.bfloat16)
            row_delta = jnp.sum(d_heads * attended.astype(jnp.float32).reshape(TOK_DEV, HEADS, HEAD_DIM), axis=2).T
            d_probs = jnp.einsum('qhd,khd->hqk', d_heads, v_heads)
            d_scores = (score_scale * weights_f * (d_probs - row_delta[:, :, None])).astype(jnp.bfloat16)
            d_scores_f = d_scores.astype(jnp.float32)
            q_grad = jnp.einsum('hqk,khd->qhd', d_scores_f, k_heads).reshape(TOK_DEV, D)
            k_part = jnp.einsum('hqk,qhd->khd', d_scores_f, q_heads).reshape(window, D)
            v_part = jnp.einsum('hqk,qhd->khd', weights_f, d_heads).reshape(window, D)
            k_grads = lax.dynamic_update_slice_in_dim(k_grads, lax.dynamic_slice_in_dim(k_grads, start, window, 0) + k_part, start, 0)
            v_grads = lax.dynamic_update_slice_in_dim(v_grads, lax.dynamic_slice_in_dim(v_grads, start, window, 0) + v_part, start, 0)
            w_grad = w_grad + jnp.dot(attended.T, dy_blk, preferred_element_type=jnp.float32)
            return (k_grads, v_grads, w_grad), q_grad

        init = (jnp.zeros((TOKENS + 2 * pad_rows, D), jnp.float32), jnp.zeros((TOKENS + 2 * pad_rows, D), jnp.float32), jnp.zeros((D, D), jnp.float32))
        finals, q_blocks = lax.scan(block_step, init, jnp.arange(TOKENS // TOK_DEV, dtype=jnp.int32))
        k_grads, v_grads, w_grad = finals
        return q_blocks.reshape(TOKENS, D), k_grads[pad_rows:pad_rows + TOKENS], v_grads[pad_rows:pad_rows + TOKENS], w_grad

    query_grad, key_grad, value_grad, w_grads = lax.map(one_group, (queries, keys, values, out_grad, lengths))
    weight_grad = jnp.sum(w_grads, axis=0) * (ALL_TOK ** -0.5)
    return query_grad, key_grad, value_grad, weight_grad
```

```python
import functools
import math

import jax
import jax.numpy as jnp
from jax import lax
from jax.experimental import pallas as pl
from jax.experimental.pallas import tpu as pltpu
from jax.sharding import PartitionSpec as P

HEADS = 16
HEAD_DIM = 72
MAXLEN = 384


NEG_FILL = -1e30


def shifted(block, axis, distance):
    devices = range(lax.axis_size(axis))
    route = [(i - distance, i) for i in devices if i - distance in devices]
    return lax.ppermute(block, axis, route)


def split_heads(rows_in):
    return rows_in.reshape(rows_in.shape[0], HEADS, HEAD_DIM)


def image_ids(image_ends, shard, tok_rows, shards):
    positions = shard * tok_rows + jnp.arange(tok_rows, dtype=jnp.int32)
    found = jnp.sum((positions[:, None] >= image_ends[None, :]).astype(jnp.int32), axis=1)
    inside = jnp.logical_and(shard >= 0, shard < shards)
    return jnp.where(inside, found, -1)


def masked_scores(q_rows, k_rows, q_ids, k_ids):
    scores = jnp.einsum(
        "qhd,khd->hqk", split_heads(q_rows), split_heads(k_rows), preferred_element_type=jnp.float32
    ) * HEAD_DIM ** (-0.5)
    same_image = q_ids[:, None] == k_ids[None, :]
    return jnp.where(same_image[None, :, :], scores, NEG_FILL)


def touches(q_ids, k_ids):
    return jnp.any(q_ids[:, None] == k_ids[None, :])


def make_probs(q_rows, k_rows, q_ids, k_ids, log_norm):
    return jnp.exp(masked_scores(q_rows, k_rows, q_ids, k_ids) - log_norm[:, :, None]).astype(
        jnp.bfloat16
    )


def score_grads(q_rows, k_rows, v_rows, d_rows, q_ids, k_ids, log_norm, row_delta):
    weights = make_probs(q_rows, k_rows, q_ids, k_ids, log_norm)
    d_probs = jnp.einsum(
        "qhd,khd->hqk", split_heads(d_rows), split_heads(v_rows), preferred_element_type=jnp.float32
    )
    d_scores = (
        HEAD_DIM ** (-0.5) * weights.astype(jnp.float32) * (d_probs - row_delta[:, :, None])
    ).astype(jnp.bfloat16)
    return (weights, d_scores)


def query_part(d_scores, k_rows):
    return jnp.einsum(
        "hqk,khd->qhd", d_scores, split_heads(k_rows), preferred_element_type=jnp.float32
    )


def key_part(weights, d_scores, q_rows, d_rows):
    k_part = jnp.einsum(
        "hqk,qhd->khd", d_scores, split_heads(q_rows), preferred_element_type=jnp.float32
    )
    v_part = jnp.einsum(
        "hqk,qhd->khd", weights, split_heads(d_rows), preferred_element_type=jnp.float32
    )
    return (k_part, v_part)


def halo_body(queries, keys, values, out_weight, out_grad, lengths):
    q_rows = queries[0]
    k_rows = keys[0]
    v_rows = values[0]
    dy_rows = out_grad[0]
    tok_rows = q_rows.shape[0]
    feature_width = q_rows.shape[1]
    shards = lax.axis_size("seq")
    seq_index = lax.axis_index("seq")
    key_reach = (MAXLEN + tok_rows - 2) // tok_rows
    image_ends = jnp.cumsum(lengths[0])
    own_ids = image_ids(image_ends, seq_index, tok_rows, shards)
    d_out = jnp.einsum("td,ed->te", dy_rows, out_weight, preferred_element_type=jnp.float32).astype(
        jnp.bfloat16
    )
    remote = []
    for distance in range(1, key_reach + 1):
        for offset in (distance, -distance):
            arrived = shifted((k_rows, v_rows), "seq", offset)
            remote.append((offset, arrived[0], arrived[1]))
    remote_ids = [image_ids(image_ends, seq_index - entry[0], tok_rows, shards) for entry in remote]
    own_scores = masked_scores(q_rows, k_rows, own_ids, own_ids)
    row_max = jnp.max(own_scores, axis=2)
    row_sum = jnp.sum(jnp.exp(own_scores - row_max[:, :, None]), axis=2)
    for entry, tile_ids in zip(remote, remote_ids):
        k_tile = entry[1]

        def widen(carried):
            old_max, old_sum = carried
            scores = masked_scores(q_rows, k_tile, own_ids, tile_ids)
            new_max = jnp.maximum(old_max, jnp.max(scores, axis=2))
            new_sum = old_sum * jnp.exp(old_max - new_max) + jnp.sum(
                jnp.exp(scores - new_max[:, :, None]), axis=2
            )
            return (new_max, new_sum)

        row_max, row_sum = lax.cond(
            touches(own_ids, tile_ids), widen, lambda carried: carried, (row_max, row_sum)
        )
    log_norm = row_max + jnp.log(row_sum)
    head_zeros = jnp.zeros((tok_rows, HEADS, HEAD_DIM), jnp.float32)
    mixed_sum = jnp.einsum(
        "hqk,khd->qhd",
        make_probs(q_rows, k_rows, own_ids, own_ids, log_norm),
        split_heads(v_rows),
        preferred_element_type=jnp.float32,
    )
    for entry, tile_ids in zip(remote, remote_ids):
        k_tile = entry[1]
        v_tile = entry[2]

        def mix_tile():
            weights = make_probs(q_rows, k_tile, own_ids, tile_ids, log_norm)
            return jnp.einsum(
                "hqk,khd->qhd", weights, split_heads(v_tile), preferred_element_type=jnp.float32
            )

        mixed_sum = mixed_sum + lax.cond(touches(own_ids, tile_ids), mix_tile, lambda: head_zeros)
    attended = mixed_sum.reshape(tok_rows, feature_width).astype(jnp.bfloat16)
    row_delta = jnp.sum(
        (d_out.astype(jnp.float32) * attended.astype(jnp.float32)).reshape(
            tok_rows, HEADS, HEAD_DIM
        ),
        axis=2,
    ).T
    weights, d_scores = score_grads(
        q_rows, k_rows, v_rows, d_out, own_ids, own_ids, log_norm, row_delta
    )
    q_grad = query_part(d_scores, k_rows)
    k_grad, v_grad = key_part(weights, d_scores, q_rows, d_out)
    for entry, tile_ids in zip(remote, remote_ids):
        offset = entry[0]
        k_tile = entry[1]
        v_tile = entry[2]

        def all_parts():
            tile_weights, tile_scores = score_grads(
                q_rows, k_tile, v_tile, d_out, own_ids, tile_ids, log_norm, row_delta
            )
            k_part, v_part = key_part(tile_weights, tile_scores, q_rows, d_out)
            return (query_part(tile_scores, k_tile), k_part, v_part)

        parts = lax.cond(
            touches(own_ids, tile_ids), all_parts, lambda: (head_zeros, head_zeros, head_zeros)
        )
        q_grad = q_grad + parts[0]
        returned = shifted(
            (parts[1].reshape(tok_rows, feature_width), parts[2].reshape(tok_rows, feature_width)),
            "seq",
            -offset,
        )
        k_grad = k_grad + returned[0].reshape(tok_rows, HEADS, HEAD_DIM)
        v_grad = v_grad + returned[1].reshape(tok_rows, HEADS, HEAD_DIM)
    weight_share = lax.psum_scatter(
        jnp.einsum("tr,tc->rc", attended, dy_rows, preferred_element_type=jnp.float32),
        "seq",
        scatter_dimension=0,
        tiled=True,
    )
    weight_sum = lax.psum(weight_share, "dp")
    all_tokens = tok_rows * shards * lax.axis_size("dp")
    weight_grad = weight_sum * (1.0 / math.sqrt(all_tokens))
    return (
        q_grad.reshape(1, tok_rows, feature_width),
        k_grad.reshape(1, tok_rows, feature_width),
        v_grad.reshape(1, tok_rows, feature_width),
        weight_grad,
    )


BF16, F32 = jnp.bfloat16, jnp.float32
ANY = pl.BlockSpec(memory_space=pl.ANY)
VMEM = pl.BlockSpec(memory_space=pltpu.VMEM)
HBM = pl.BlockSpec(memory_space=pltpu.HBM)
SMEM = pl.BlockSpec(memory_space=pltpu.SMEM)
DMA = pltpu.SemaphoreType.DMA
PARAMS = pltpu.CompilerParams(vmem_limit_bytes=16 * 1024 * 1024)
NT = ((1,), (1,))


def dot(a, b, contract=((1,), (0,))):
    return lax.dot_general(a, b, (contract, ((), ())), preferred_element_type=F32)


def spread_kernel(q_ref, k_ref, v_ref, out_ref, rows_s, turned_s, in_sem, out_sem):
    shards, height, _ = out_ref.shape
    part = height // 3
    loads = [pltpu.make_async_copy(ref, rows_s.at[i], in_sem.at[i]) for i, ref in enumerate((q_ref, k_ref, v_ref))]
    for load in loads:
        load.start()
    stores = []
    for i, load in enumerate(loads):
        load.wait()
        turned = rows_s[i].T
        for shard in range(shards):
            turned_s[i, shard] = turned[shard * part:(shard + 1) * part, :]
        store = pltpu.make_async_copy(turned_s.at[i], out_ref.at[:, pl.ds(i * part, part), :], out_sem.at[i])
        store.start()
        stores.append(store)
    for store in stores:
        store.wait()


def collect_kernel(*refs):
    blocks, (q_ref, k_ref, v_ref, turned_s, rows_s, out_sem) = refs[:-6], refs[-6:]
    part = blocks[0].shape[0] // 3
    me = lax.axis_index("seq")
    for n, block in enumerate(blocks):
        turned_s[me ^ (-n % len(blocks))] = block[...]
    stores = []
    for i, ref in enumerate((q_ref, k_ref, v_ref)):
        whole = jnp.concatenate([turned_s[n, i * part:(i + 1) * part, :] for n in range(len(blocks))], axis=0)
        rows_s[i] = whole.astype(F32).T
        store = pltpu.make_async_copy(rows_s.at[i], ref, out_sem.at[i])
        store.start()
        stores.append(store)
    for store in stores:
        store.wait()


def window_sizes(tok, shards):
    return min(2, shards), min((MAXLEN + tok - 2) // tok + 1, shards)


def each_image(lengths, tok, shards, work):
    least, most = window_sizes(tok, shards)

    def one_image(image, start):
        end = start + lengths[0, image]
        low = start // tok
        count = jnp.maximum((end - 1) // tok - low + 1, least)
        first = jnp.minimum(low, shards - count)
        for size in range(least, most + 1):
            @pl.when(count == size)
            def _():
                work(image, size, first, start, end)
        return end

    lax.fori_loop(0, lengths.shape[1], one_image, jnp.int32(0))


def store_heads(ref, block, columns):
    heads, padded, _ = ref.shape
    filler = jnp.zeros((padded - HEAD_DIM, block.shape[1]), F32)
    for head in range(heads):
        rows = block[head * HEAD_DIM:(head + 1) * HEAD_DIM, :]
        ref[head, :, columns] = jnp.concatenate([rows, filler], axis=0).astype(BF16)


def joined(ref):
    return jnp.concatenate([ref[head, 0:HEAD_DIM, :] for head in range(ref.shape[0])], axis=0).astype(BF16)


def forward_kernel(early, len_ref, w_ref, in_ref, *refs):
    pieces = refs[:early]
    (q_s, k_s, vt_s, att_s, probs_s, d_s, wg_s, w_s, len_s, v_s, kt_s, sum_s, dy_s, len_sem, w_sem, dy_sem) = refs[early:]
    shards, height, tok = in_ref.shape
    part = height // 3
    heads = q_s.shape[0]
    scale = HEAD_DIM ** (-0.5)

    load_len = pltpu.make_async_copy(len_ref, len_s, len_sem)
    load_len.start()
    load_w = load_w_rows(w_ref, w_s, w_sem)
    loads = load_rows(pieces, dy_s, dy_sem)
    sum_s[...] = jnp.zeros_like(sum_s)
    for shard in range(shards):
        columns = slice(shard * tok, (shard + 1) * tok)
        for i, ref in enumerate((q_s, k_s, v_s)):
            store_heads(ref, in_ref[shard, i * part:(i + 1) * part, :].astype(F32), columns)
    for head in range(heads):
        kt_s[head] = k_s[head].T
        vt_s[head] = v_s[head].T
    load_len.wait()

    def work(image, count, first, start, end):
        width = count * tok
        base = pl.multiple_of(first * tok, tok)
        columns = pl.ds(base, width)
        key_pos = base + lax.broadcasted_iota(jnp.int32, (width, 1), 0)
        key_in = jnp.logical_and(key_pos >= start, key_pos < end)
        query_pos = base + lax.broadcasted_iota(jnp.int32, (1, width), 1)
        query_in = jnp.logical_and(query_pos >= start, query_pos < end)
        for head in range(heads):
            scores = jnp.where(key_in, dot(kt_s[head, columns, :], q_s[head, :, columns]), NEG_FILL)
            top = jnp.max(scores, axis=0, keepdims=True)
            grown = jnp.exp((scores - top) * scale)
            total = jnp.sum(grown, axis=0, keepdims=True)
            probs = (grown * jnp.where(query_in, 1.0 / total, 0.0)).astype(BF16)
            probs_s[image, head, 0:width, 0:width] = probs
            sum_s[head, :, columns] += dot(v_s[head, :, columns], probs)

    each_image(len_s, tok, shards, work)
    att_s[...] = joined(sum_s)
    for n in range(early, shards):
        dy_s[piece_columns(n, tok), :] = jnp.zeros((tok, dy_s.shape[1]), BF16)
    load_w.wait()
    for load in loads:
        load.wait()
    for shard in range(0, shards, 2):
        d_block = dot(w_s[...], dy_s[shard * tok:(shard + 2) * tok, :], NT)
        store_heads(d_s, d_block, slice(shard * tok, (shard + 2) * tok))
    wg_s[...] = dot(att_s[...], dy_s[...])


def backward_kernel(early, len_ref, w_s, q_s, k_s, vt_s, att_s, probs_s, d_ref, *refs):
    late = refs[:8 - early]
    outs = refs[8 - early:16 - early]
    (len_s, d_s, dq_s, dk_s, dv_s, out_s, len_sem, out_sem) = refs[16 - early:]
    shards, height, tok = out_s.shape
    part = height // 3
    heads = d_s.shape[0]
    scale = HEAD_DIM ** (-0.5)
    load_len = pltpu.make_async_copy(len_ref, len_s, len_sem)
    load_len.start()
    d_s[...] = d_ref[...]
    for ref in (dq_s, dk_s, dv_s):
        ref[...] = jnp.zeros_like(ref)
    for n, piece in enumerate(late):
        store_heads(d_s, dot(w_s[...], piece[...], NT), piece_columns(early + n, tok))
    load_len.wait()

    def work(image, count, first, start, end):
        width = count * tok
        columns = pl.ds(pl.multiple_of(first * tok, tok), width)
        att_all = att_s[:, columns].astype(F32)
        for head in range(heads):
            d = d_s[head, :, columns]
            probs = probs_s[image, head, 0:width, 0:width]
            att = att_all[head * HEAD_DIM:(head + 1) * HEAD_DIM, :]
            delta = jnp.sum(d[0:HEAD_DIM, :].astype(F32) * att, axis=0, keepdims=True)
            d_probs = dot(vt_s[head, columns, :], d)
            d_scores = (scale * probs.astype(F32) * (d_probs - delta)).astype(BF16)
            dq_s[head, :, columns] += dot(k_s[head, :, columns], d_scores)
            dk_s[head, :, columns] += dot(q_s[head, :, columns], d_scores, NT)
            dv_s[head, :, columns] += dot(d, probs, NT)

    each_image(len_s, tok, shards, work)

    stores = []
    for i, ref in enumerate((dq_s, dk_s, dv_s)):
        whole = joined(ref)
        for shard in range(shards):
            out_s[shard, i * part:(i + 1) * part, :] = whole[:, shard * tok:(shard + 1) * tok]
    me = lax.axis_index("seq")
    for n in range(shards - 1, 0, -1):
        store = pltpu.make_async_copy(out_s.at[me ^ n], outs[n], out_sem.at[n])
        store.start()
        stores.append(store)
    outs[0][...] = out_s[me]
    for store in stores:
        store.wait()


def weight_kernel(early, att_ref, wg_ref, *refs):
    late, out_ref = refs[:-1], refs[-1]
    total = wg_ref[...]
    for n, piece in enumerate(late):
        total = total + dot(att_ref[:, piece_columns(early + n, piece.shape[0])], piece[...])
    out_ref[...] = total.astype(BF16)


def load_w_rows(w_ref, w_s, sem):
    part = w_s.shape[0]
    row = pl.multiple_of(lax.axis_index("seq") * part, part)
    load = pltpu.make_async_copy(w_ref.at[pl.ds(row, part), :], w_s, sem)
    load.start()
    return load


def piece_columns(n, tok):
    me = lax.axis_index("seq")
    owner = me ^ jnp.where(is_inner(me), INNER_SOURCES[n], OUTER_SOURCES[n])
    return pl.ds(pl.multiple_of(owner * tok, tok), tok)


def load_rows(pieces, dy_s, sems):
    loads = []
    for n, piece in enumerate(pieces):
        load = pltpu.make_async_copy(piece, dy_s.at[piece_columns(n, piece.shape[0]), :], sems.at[n])
        load.start()
        loads.append(load)
    return loads


INNER_SOURCES = (0, 2, 6, 4, 3, 1, 7, 5)
OUTER_SOURCES = (0, 2, 1, 3, 4, 6, 5, 7)


def is_inner(index):
    z = index // 2
    return jnp.logical_or(z == 1, z == 2)


def gather_steps(block, event):
    devices = range(8)
    along = [(i, i ^ 2) for i in devices]
    across = [(i, i ^ 1) for i in devices]
    middle = [(i, i ^ 6 if i // 2 in (1, 2) else i ^ 1) for i in devices]
    inner = is_inner(lax.axis_index("seq"))

    def move(value, pairs):
        return lax.ppermute(value, "seq", pairs)

    one = move(block, along)
    two = move(block, middle)
    one, two = after(one, event), after(two, event)
    three = move(one, middle)
    four = move(two, along)
    five = move(three, along)
    six = move(jnp.where(inner, two, four), across)
    seven = move(jnp.where(inner, three, five), across)
    return (block, one, two, three, four, five, six, seven)


def after(value, *events):
    return lax.optimization_barrier((value, *events))[0]


def in_hbm(*arrays):
    return [pltpu.with_memory_space_constraint(array, pltpu.HBM) for array in arrays]


def head_body(queries, keys, values, out_weight, out_grad, lengths):
    tok, width = queries.shape[1:]
    shards = lax.axis_size("seq")
    groups = lax.axis_size("dp")
    part = width // shards
    heads = HEADS // shards
    tokens = tok * shards
    padded = -(-HEAD_DIM // 16) * 16

    def shape(dims, kind=BF16):
        return jax.ShapeDtypeStruct(dims, kind)

    sent = pl.pallas_call(
        spread_kernel, out_shape=pltpu.HBM((shards, 3 * part, tok), BF16),
        in_specs=[HBM] * 3, out_specs=HBM, compiler_params=PARAMS,
        scratch_shapes=[pltpu.VMEM((3, tok, width), BF16), pltpu.VMEM((3, shards, part, tok), BF16), DMA((3,)), DMA((3,))],
    )(*in_hbm(queries[0], keys[0], values[0]))
    pieces = gather_steps(out_grad[0], sent)
    arrived = lax.all_to_all(after(sent, *pieces[1:3]), "seq", 0, 0, tiled=True)

    images = lengths.shape[1]
    window = window_sizes(tok, shards)[1] * tok
    wide, tall = (heads, padded, tokens), (heads, tokens, padded)
    flat, chance = (part, tokens), (images, heads, window, window)

    def scratch(*dims, kind=BF16):
        return [pltpu.VMEM(d, kind) for d in dims]

    len_s = pltpu.SMEM((1, images), jnp.int32)
    early = 6
    late = len(pieces) - early
    q_t, k_t, v_r, attended, probs, d_part, w_early, w_rows = pl.pallas_call(
        functools.partial(forward_kernel, early),
        out_shape=[shape(wide), shape(wide), shape(tall), shape(flat), shape(chance), shape(wide), shape((part, width), F32), shape((part, width))],
        in_specs=[HBM, HBM, VMEM] + [HBM] * early, out_specs=[VMEM] * 8, compiler_params=PARAMS,
        scratch_shapes=[len_s] + scratch(wide, tall) + scratch(wide, kind=F32) + scratch((tokens, width))
        + [DMA, DMA, DMA((early,))],
    )(*in_hbm(lengths, out_weight), arrived, *in_hbm(*pieces[:early]))
    w_part = pl.pallas_call(
        functools.partial(weight_kernel, early), out_shape=shape((part, width)),
        in_specs=[VMEM] * (2 + late), out_specs=VMEM, compiler_params=PARAMS,
    )(attended, w_early, *pieces[early:])
    grads = pl.pallas_call(
        functools.partial(backward_kernel, early),
        out_shape=[shape((3 * part, tok))] + [pltpu.HBM((3 * part, tok), BF16)] * (shards - 1),
        in_specs=[HBM] + [VMEM] * (7 + late), out_specs=[VMEM] + [HBM] * (shards - 1), compiler_params=PARAMS,
        scratch_shapes=[len_s] + scratch(wide) + scratch(wide, wide, wide, kind=F32)
        + scratch((shards, 3 * part, tok)) + [DMA, DMA((shards,))],
    )(*in_hbm(lengths), w_rows, q_t, k_t, v_r, attended, probs, d_part, *pieces[early:])
    sums = w_part.astype(F32)
    step = 1
    while step < groups:
        pairs = [(i, i ^ step) for i in range(groups)]
        sums = w_part.astype(F32) + after(lax.ppermute(w_part, "dp", pairs), grads[0]).astype(F32)
        w_part = lax.reduce_precision(sums, 8, 7).astype(BF16)
        step *= 2
    weight_grad = sums * (1.0 / math.sqrt(tokens * groups))

    returned = [grads[0]]
    for n in range(shards - 1, 0, -1):
        block = grads[n] if n > 1 else after(grads[n], weight_grad)
        returned.append(lax.ppermute(block, "seq", [(i, i ^ n) for i in range(shards)]))
    q_grad, k_grad, v_grad = pl.pallas_call(
        collect_kernel, out_shape=[shape((tok, width), F32)] * 3, in_specs=[VMEM] * shards, out_specs=[ANY] * 3,
        compiler_params=PARAMS,
        scratch_shapes=scratch((shards, 3 * part, tok)) + scratch((3, tok, width), kind=F32) + [DMA((3,))],
    )(*returned)
    return q_grad[None], k_grad[None], v_grad[None], weight_grad


def solution(mesh):
    in_specs = (
        P("dp", "seq", None),
        P("dp", "seq", None),
        P("dp", "seq", None),
        P(),
        P("dp", "seq", None),
        P("dp", None),
    )
    out_specs = (P("dp", "seq", None), P("dp", "seq", None), P("dp", "seq", None), P("seq", None))
    by_heads = mesh.shape["seq"] == 8 and mesh.shape["dp"] & (mesh.shape["dp"] - 1) == 0
    body = head_body if by_heads else halo_body
    return jax.shard_map(body, mesh=mesh, in_specs=in_specs, out_specs=out_specs, check_vma=False)
```

```python
import functools
import math

import jax
import jax.numpy as jnp
from jax import lax
from jax.experimental import pallas as pl
from jax.experimental.pallas import tpu as pltpu
from jax.sharding import PartitionSpec as P

HEADS = 16
HEAD_DIM = 72
MAXLEN = 384


NEG_FILL = -1e30


def shifted(block, axis, distance):
    devices = range(lax.axis_size(axis))
    route = [(i - distance, i) for i in devices if i - distance in devices]
    return lax.ppermute(block, axis, route)


def split_heads(rows_in):
    return rows_in.reshape(rows_in.shape[0], HEADS, HEAD_DIM)


def image_ids(image_ends, shard, tok_rows, shards):
    positions = shard * tok_rows + jnp.arange(tok_rows, dtype=jnp.int32)
    found = jnp.sum((positions[:, None] >= image_ends[None, :]).astype(jnp.int32), axis=1)
    inside = jnp.logical_and(shard >= 0, shard < shards)
    return jnp.where(inside, found, -1)


def masked_scores(q_rows, k_rows, q_ids, k_ids):
    scores = jnp.einsum(
        "qhd,khd->hqk", split_heads(q_rows), split_heads(k_rows), preferred_element_type=jnp.float32
    ) * HEAD_DIM ** (-0.5)
    same_image = q_ids[:, None] == k_ids[None, :]
    return jnp.where(same_image[None, :, :], scores, NEG_FILL)


def touches(q_ids, k_ids):
    return jnp.any(q_ids[:, None] == k_ids[None, :])


def make_probs(q_rows, k_rows, q_ids, k_ids, log_norm):
    return jnp.exp(masked_scores(q_rows, k_rows, q_ids, k_ids) - log_norm[:, :, None]).astype(
        jnp.bfloat16
    )


def score_grads(q_rows, k_rows, v_rows, d_rows, q_ids, k_ids, log_norm, row_delta):
    weights = make_probs(q_rows, k_rows, q_ids, k_ids, log_norm)
    d_probs = jnp.einsum(
        "qhd,khd->hqk", split_heads(d_rows), split_heads(v_rows), preferred_element_type=jnp.float32
    )
    d_scores = (
        HEAD_DIM ** (-0.5) * weights.astype(jnp.float32) * (d_probs - row_delta[:, :, None])
    ).astype(jnp.bfloat16)
    return (weights, d_scores)


def query_part(d_scores, k_rows):
    return jnp.einsum(
        "hqk,khd->qhd", d_scores, split_heads(k_rows), preferred_element_type=jnp.float32
    )


def key_part(weights, d_scores, q_rows, d_rows):
    k_part = jnp.einsum(
        "hqk,qhd->khd", d_scores, split_heads(q_rows), preferred_element_type=jnp.float32
    )
    v_part = jnp.einsum(
        "hqk,qhd->khd", weights, split_heads(d_rows), preferred_element_type=jnp.float32
    )
    return (k_part, v_part)


def halo_body(queries, keys, values, out_weight, out_grad, lengths):
    q_rows = queries[0]
    k_rows = keys[0]
    v_rows = values[0]
    dy_rows = out_grad[0]
    tok_rows = q_rows.shape[0]
    feature_width = q_rows.shape[1]
    shards = lax.axis_size("seq")
    seq_index = lax.axis_index("seq")
    key_reach = (MAXLEN + tok_rows - 2) // tok_rows
    image_ends = jnp.cumsum(lengths[0])
    own_ids = image_ids(image_ends, seq_index, tok_rows, shards)
    d_out = jnp.einsum("td,ed->te", dy_rows, out_weight, preferred_element_type=jnp.float32).astype(
        jnp.bfloat16
    )
    remote = []
    for distance in range(1, key_reach + 1):
        for offset in (distance, -distance):
            arrived = shifted((k_rows, v_rows), "seq", offset)
            remote.append((offset, arrived[0], arrived[1]))
    remote_ids = [image_ids(image_ends, seq_index - entry[0], tok_rows, shards) for entry in remote]
    own_scores = masked_scores(q_rows, k_rows, own_ids, own_ids)
    row_max = jnp.max(own_scores, axis=2)
    row_sum = jnp.sum(jnp.exp(own_scores - row_max[:, :, None]), axis=2)
    for entry, tile_ids in zip(remote, remote_ids):
        k_tile = entry[1]

        def widen(carried):
            old_max, old_sum = carried
            scores = masked_scores(q_rows, k_tile, own_ids, tile_ids)
            new_max = jnp.maximum(old_max, jnp.max(scores, axis=2))
            new_sum = old_sum * jnp.exp(old_max - new_max) + jnp.sum(
                jnp.exp(scores - new_max[:, :, None]), axis=2
            )
            return (new_max, new_sum)

        row_max, row_sum = lax.cond(
            touches(own_ids, tile_ids), widen, lambda carried: carried, (row_max, row_sum)
        )
    log_norm = row_max + jnp.log(row_sum)
    head_zeros = jnp.zeros((tok_rows, HEADS, HEAD_DIM), jnp.float32)
    mixed_sum = jnp.einsum(
        "hqk,khd->qhd",
        make_probs(q_rows, k_rows, own_ids, own_ids, log_norm),
        split_heads(v_rows),
        preferred_element_type=jnp.float32,
    )
    for entry, tile_ids in zip(remote, remote_ids):
        k_tile = entry[1]
        v_tile = entry[2]

        def mix_tile():
            weights = make_probs(q_rows, k_tile, own_ids, tile_ids, log_norm)
            return jnp.einsum(
                "hqk,khd->qhd", weights, split_heads(v_tile), preferred_element_type=jnp.float32
            )

        mixed_sum = mixed_sum + lax.cond(touches(own_ids, tile_ids), mix_tile, lambda: head_zeros)
    attended = mixed_sum.reshape(tok_rows, feature_width).astype(jnp.bfloat16)
    row_delta = jnp.sum(
        (d_out.astype(jnp.float32) * attended.astype(jnp.float32)).reshape(
            tok_rows, HEADS, HEAD_DIM
        ),
        axis=2,
    ).T
    weights, d_scores = score_grads(
        q_rows, k_rows, v_rows, d_out, own_ids, own_ids, log_norm, row_delta
    )
    q_grad = query_part(d_scores, k_rows)
    k_grad, v_grad = key_part(weights, d_scores, q_rows, d_out)
    for entry, tile_ids in zip(remote, remote_ids):
        offset = entry[0]
        k_tile = entry[1]
        v_tile = entry[2]

        def all_parts():
            tile_weights, tile_scores = score_grads(
                q_rows, k_tile, v_tile, d_out, own_ids, tile_ids, log_norm, row_delta
            )
            k_part, v_part = key_part(tile_weights, tile_scores, q_rows, d_out)
            return (query_part(tile_scores, k_tile), k_part, v_part)

        parts = lax.cond(
            touches(own_ids, tile_ids), all_parts, lambda: (head_zeros, head_zeros, head_zeros)
        )
        q_grad = q_grad + parts[0]
        returned = shifted(
            (parts[1].reshape(tok_rows, feature_width), parts[2].reshape(tok_rows, feature_width)),
            "seq",
            -offset,
        )
        k_grad = k_grad + returned[0].reshape(tok_rows, HEADS, HEAD_DIM)
        v_grad = v_grad + returned[1].reshape(tok_rows, HEADS, HEAD_DIM)
    weight_share = lax.psum_scatter(
        jnp.einsum("tr,tc->rc", attended, dy_rows, preferred_element_type=jnp.float32),
        "seq",
        scatter_dimension=0,
        tiled=True,
    )
    weight_sum = lax.psum(weight_share, "dp")
    all_tokens = tok_rows * shards * lax.axis_size("dp")
    weight_grad = weight_sum * (1.0 / math.sqrt(all_tokens))
    return (
        q_grad.reshape(1, tok_rows, feature_width),
        k_grad.reshape(1, tok_rows, feature_width),
        v_grad.reshape(1, tok_rows, feature_width),
        weight_grad,
    )


BF16, F32 = jnp.bfloat16, jnp.float32
ANY = pl.BlockSpec(memory_space=pl.ANY)
VMEM = pl.BlockSpec(memory_space=pltpu.VMEM)
HBM = pl.BlockSpec(memory_space=pltpu.HBM)
SMEM = pl.BlockSpec(memory_space=pltpu.SMEM)
DMA = pltpu.SemaphoreType.DMA
PARAMS = pltpu.CompilerParams(vmem_limit_bytes=16 * 1024 * 1024)
NT = ((1,), (1,))


def dot(a, b, contract=((1,), (0,))):
    return lax.dot_general(a, b, (contract, ((), ())), preferred_element_type=F32)


def spread_kernel(q_ref, k_ref, v_ref, out_ref, rows_s, turned_s, in_sem, out_sem):
    shards, height, _ = out_ref.shape
    part = height // 3
    loads = [pltpu.make_async_copy(ref, rows_s.at[i], in_sem.at[i]) for i, ref in enumerate((q_ref, k_ref, v_ref))]
    for load in loads:
        load.start()
    stores = []
    for i, load in enumerate(loads):
        load.wait()
        turned = rows_s[i].T
        for shard in range(shards):
            turned_s[i, shard] = turned[shard * part:(shard + 1) * part, :]
        store = pltpu.make_async_copy(turned_s.at[i], out_ref.at[:, pl.ds(i * part, part), :], out_sem.at[i])
        store.start()
        stores.append(store)
    for store in stores:
        store.wait()


def collect_kernel(*refs):
    blocks, (q_ref, k_ref, v_ref, turned_s, rows_s, out_sem) = refs[:-6], refs[-6:]
    part = blocks[0].shape[0] // 3
    me = lax.axis_index("seq")
    for n, block in enumerate(blocks):
        turned_s[me ^ BACK_ORDER[n]] = block[...]
    stores = []
    for i, ref in enumerate((q_ref, k_ref, v_ref)):
        whole = jnp.concatenate([turned_s[n, i * part:(i + 1) * part, :] for n in range(len(blocks))], axis=0)
        rows_s[i] = whole.astype(F32).T
        store = pltpu.make_async_copy(rows_s.at[i], ref, out_sem.at[i])
        store.start()
        stores.append(store)
    for store in stores:
        store.wait()


def window_sizes(tok, shards):
    return min(2, shards), min((MAXLEN + tok - 2) // tok + 1, shards)


def each_image(lengths, tok, shards, work):
    least, most = window_sizes(tok, shards)

    def one_image(image, start):
        end = start + lengths[0, image]
        low = start // tok
        count = jnp.maximum((end - 1) // tok - low + 1, least)
        first = jnp.minimum(low, shards - count)
        for size in range(least, most + 1):
            @pl.when(count == size)
            def _():
                work(image, size, first, start, end)
        return end

    lax.fori_loop(0, lengths.shape[1], one_image, jnp.int32(0))


def store_heads(ref, block, columns):
    heads, padded, _ = ref.shape
    filler = jnp.zeros((padded - HEAD_DIM, block.shape[1]), F32)
    for head in range(heads):
        rows = block[head * HEAD_DIM:(head + 1) * HEAD_DIM, :]
        ref[head, :, columns] = jnp.concatenate([rows, filler], axis=0).astype(BF16)


def joined(ref):
    return jnp.concatenate([ref[head, 0:HEAD_DIM, :] for head in range(ref.shape[0])], axis=0).astype(BF16)


def forward_kernel(early, len_ref, w_ref, in_ref, *refs):
    pieces = refs[:early]
    (q_s, k_s, vt_s, att_s, probs_s, d_s, wg_s, w_s, len_s, v_s, kt_s, sum_s, dy_s, len_sem, w_sem, dy_sem) = refs[early:]
    shards, height, tok = in_ref.shape
    part = height // 3
    heads = q_s.shape[0]
    scale = HEAD_DIM ** (-0.5)

    load_len = pltpu.make_async_copy(len_ref, len_s, len_sem)
    load_len.start()
    load_w = load_w_rows(w_ref, w_s, w_sem)
    loads = load_rows(pieces, dy_s, dy_sem)
    sum_s[...] = jnp.zeros_like(sum_s)
    for shard in range(shards):
        columns = slice(shard * tok, (shard + 1) * tok)
        for i, ref in enumerate((q_s, k_s, v_s)):
            store_heads(ref, in_ref[shard, i * part:(i + 1) * part, :].astype(F32), columns)
    for head in range(heads):
        kt_s[head] = k_s[head].T
        vt_s[head] = v_s[head].T
    load_len.wait()

    def work(image, count, first, start, end):
        width = count * tok
        base = pl.multiple_of(first * tok, tok)
        columns = pl.ds(base, width)
        key_pos = base + lax.broadcasted_iota(jnp.int32, (width, 1), 0)
        key_in = jnp.logical_and(key_pos >= start, key_pos < end)
        query_pos = base + lax.broadcasted_iota(jnp.int32, (1, width), 1)
        query_in = jnp.logical_and(query_pos >= start, query_pos < end)
        for head in range(heads):
            scores = jnp.where(key_in, dot(kt_s[head, columns, :], q_s[head, :, columns]), NEG_FILL)
            top = jnp.max(scores, axis=0, keepdims=True)
            grown = jnp.exp((scores - top) * scale)
            total = jnp.sum(grown, axis=0, keepdims=True)
            probs = (grown * jnp.where(query_in, 1.0 / total, 0.0)).astype(BF16)
            probs_s[image, head, 0:width, 0:width] = probs
            sum_s[head, :, columns] += dot(v_s[head, :, columns], probs)

    each_image(len_s, tok, shards, work)
    att_s[...] = joined(sum_s)
    for n in range(early, shards):
        dy_s[piece_columns(n, tok), :] = jnp.zeros((tok, dy_s.shape[1]), BF16)
    load_w.wait()
    for load in loads:
        load.wait()
    for shard in range(0, shards, 2):
        d_block = dot(w_s[...], dy_s[shard * tok:(shard + 2) * tok, :], NT)
        store_heads(d_s, d_block, slice(shard * tok, (shard + 2) * tok))
    wg_s[...] = dot(att_s[...], dy_s[...])


def backward_kernel(early, len_ref, w_s, q_s, k_s, vt_s, att_s, probs_s, d_ref, *refs):
    late = refs[:8 - early]
    outs = refs[8 - early:16 - early]
    (len_s, d_s, dq_s, dk_s, dv_s, out_s, len_sem, out_sem) = refs[16 - early:]
    shards, height, tok = out_s.shape
    part = height // 3
    heads = d_s.shape[0]
    scale = HEAD_DIM ** (-0.5)
    load_len = pltpu.make_async_copy(len_ref, len_s, len_sem)
    load_len.start()
    d_s[...] = d_ref[...]
    for ref in (dq_s, dk_s, dv_s):
        ref[...] = jnp.zeros_like(ref)
    for n, piece in enumerate(late):
        store_heads(d_s, dot(w_s[...], piece[...], NT), piece_columns(early + n, tok))
    load_len.wait()

    def work(image, count, first, start, end):
        width = count * tok
        columns = pl.ds(pl.multiple_of(first * tok, tok), width)
        att_all = att_s[:, columns].astype(F32)
        for head in range(heads):
            d = d_s[head, :, columns]
            probs = probs_s[image, head, 0:width, 0:width]
            att = att_all[head * HEAD_DIM:(head + 1) * HEAD_DIM, :]
            delta = jnp.sum(d[0:HEAD_DIM, :].astype(F32) * att, axis=0, keepdims=True)
            d_probs = dot(vt_s[head, columns, :], d)
            d_scores = (scale * probs.astype(F32) * (d_probs - delta)).astype(BF16)
            dq_s[head, :, columns] += dot(k_s[head, :, columns], d_scores)
            dk_s[head, :, columns] += dot(q_s[head, :, columns], d_scores, NT)
            dv_s[head, :, columns] += dot(d, probs, NT)

    each_image(len_s, tok, shards, work)

    stores = []
    for i, ref in enumerate((dq_s, dk_s, dv_s)):
        whole = joined(ref)
        for shard in range(shards):
            out_s[shard, i * part:(i + 1) * part, :] = whole[:, shard * tok:(shard + 1) * tok]
    me = lax.axis_index("seq")
    for n in range(shards - 1, 0, -1):
        store = pltpu.make_async_copy(out_s.at[me ^ n], outs[n], out_sem.at[n])
        store.start()
        stores.append(store)
    outs[0][...] = out_s[me]
    for store in stores:
        store.wait()


def weight_kernel(early, att_ref, wg_ref, *refs):
    late, out_ref = refs[:-1], refs[-1]
    total = wg_ref[...]
    for n, piece in enumerate(late):
        total = total + dot(att_ref[:, piece_columns(early + n, piece.shape[0])], piece[...])
    out_ref[...] = total.astype(BF16)


def load_w_rows(w_ref, w_s, sem):
    part = w_s.shape[0]
    row = pl.multiple_of(lax.axis_index("seq") * part, part)
    load = pltpu.make_async_copy(w_ref.at[pl.ds(row, part), :], w_s, sem)
    load.start()
    return load


def piece_columns(n, tok):
    me = lax.axis_index("seq")
    owner = me ^ jnp.where(is_inner(me), INNER_SOURCES[n], OUTER_SOURCES[n])
    return pl.ds(pl.multiple_of(owner * tok, tok), tok)


def load_rows(pieces, dy_s, sems):
    loads = []
    for n, piece in enumerate(pieces):
        load = pltpu.make_async_copy(piece, dy_s.at[piece_columns(n, piece.shape[0]), :], sems.at[n])
        load.start()
        loads.append(load)
    return loads


BACK_ORDER = (0, 5, 3, 4, 7, 6, 2, 1)
FIFTH_PARTS = 4
INNER_SOURCES = (0, 2, 6, 4, 3, 1, 7, 5)
OUTER_SOURCES = (0, 2, 1, 3, 4, 6, 5, 7)


def is_inner(index):
    z = index // 2
    return jnp.logical_or(z == 1, z == 2)


def gather_steps(block, event):
    devices = range(8)
    along = [(i, i ^ 2) for i in devices]
    across = [(i, i ^ 1) for i in devices]
    middle = [(i, i ^ 6 if i // 2 in (1, 2) else i ^ 1) for i in devices]
    inner = is_inner(lax.axis_index("seq"))

    def move(value, pairs):
        return lax.ppermute(value, "seq", pairs)

    one = move(block, along)
    two = move(block, middle)
    one, two = after(one, event), after(two, event)
    three = move(one, middle)
    four = move(two, along)
    rows = block.shape[0] // FIFTH_PARTS
    five = jnp.concatenate([move(three[n * rows:(n + 1) * rows], along) for n in range(FIFTH_PARTS)])
    six = move(jnp.where(inner, two, four), across)
    seven = move(jnp.where(inner, three, five), across)
    return (block, one, two, three, four, five, six, seven)


def after(value, *events):
    return lax.optimization_barrier((value, *events))[0]


def in_hbm(*arrays):
    return [pltpu.with_memory_space_constraint(array, pltpu.HBM) for array in arrays]


def head_body(queries, keys, values, out_weight, out_grad, lengths):
    tok, width = queries.shape[1:]
    shards = lax.axis_size("seq")
    groups = lax.axis_size("dp")
    part = width // shards
    heads = HEADS // shards
    tokens = tok * shards
    padded = -(-HEAD_DIM // 16) * 16

    def shape(dims, kind=BF16):
        return jax.ShapeDtypeStruct(dims, kind)

    sent = pl.pallas_call(
        spread_kernel, out_shape=pltpu.HBM((shards, 3 * part, tok), BF16),
        in_specs=[HBM] * 3, out_specs=HBM, compiler_params=PARAMS,
        scratch_shapes=[pltpu.VMEM((3, tok, width), BF16), pltpu.VMEM((3, shards, part, tok), BF16), DMA((3,)), DMA((3,))],
    )(*in_hbm(queries[0], keys[0], values[0]))
    pieces = gather_steps(out_grad[0], sent)
    arrived = lax.all_to_all(after(sent, *pieces[1:3]), "seq", 0, 0, tiled=True)

    images = lengths.shape[1]
    window = window_sizes(tok, shards)[1] * tok
    wide, tall = (heads, padded, tokens), (heads, tokens, padded)
    flat, chance = (part, tokens), (images, heads, window, window)

    def scratch(*dims, kind=BF16):
        return [pltpu.VMEM(d, kind) for d in dims]

    len_s = pltpu.SMEM((1, images), jnp.int32)
    early = 6
    late = len(pieces) - early
    q_t, k_t, v_r, attended, probs, d_part, w_early, w_rows = pl.pallas_call(
        functools.partial(forward_kernel, early),
        out_shape=[shape(wide), shape(wide), shape(tall), shape(flat), shape(chance), shape(wide), shape((part, width), F32), shape((part, width))],
        in_specs=[HBM, HBM, VMEM] + [HBM] * early, out_specs=[VMEM] * 8, compiler_params=PARAMS,
        scratch_shapes=[len_s] + scratch(wide, tall) + scratch(wide, kind=F32) + scratch((tokens, width))
        + [DMA, DMA, DMA((early,))],
    )(*in_hbm(lengths, out_weight), arrived, *in_hbm(*pieces[:early]))
    w_part = pl.pallas_call(
        functools.partial(weight_kernel, early), out_shape=shape((part, width)),
        in_specs=[VMEM] * (2 + late), out_specs=VMEM, compiler_params=PARAMS,
    )(attended, w_early, *pieces[early:])
    grads = pl.pallas_call(
        functools.partial(backward_kernel, early),
        out_shape=[shape((3 * part, tok))] + [pltpu.HBM((3 * part, tok), BF16)] * (shards - 1),
        in_specs=[HBM] + [VMEM] * (7 + late), out_specs=[VMEM] + [HBM] * (shards - 1), compiler_params=PARAMS,
        scratch_shapes=[len_s] + scratch(wide) + scratch(wide, wide, wide, kind=F32)
        + scratch((shards, 3 * part, tok)) + [DMA, DMA((shards,))],
    )(*in_hbm(lengths), w_rows, q_t, k_t, v_r, attended, probs, d_part, *pieces[early:])
    sums = w_part.astype(F32)
    step = 1
    while step < groups:
        pairs = [(i, i ^ step) for i in range(groups)]
        sums = w_part.astype(F32) + after(lax.ppermute(w_part, "dp", pairs), grads[0]).astype(F32)
        w_part = lax.reduce_precision(sums, 8, 7).astype(BF16)
        step *= 2
    weight_grad = sums * (1.0 / math.sqrt(tokens * groups))

    returned = [grads[0]]
    for n in BACK_ORDER[1:]:
        block = after(grads[n], weight_grad) if n == BACK_ORDER[-1] else grads[n]
        returned.append(lax.ppermute(block, "seq", [(i, i ^ n) for i in range(shards)]))

    q_grad, k_grad, v_grad = pl.pallas_call(
        collect_kernel, out_shape=[shape((tok, width), F32)] * 3, in_specs=[VMEM] * shards, out_specs=[ANY] * 3,
        compiler_params=PARAMS,
        scratch_shapes=scratch((shards, 3 * part, tok)) + scratch((3, tok, width), kind=F32) + [DMA((3,))],
    )(*returned)
    return q_grad[None], k_grad[None], v_grad[None], weight_grad


def solution(mesh):
    in_specs = (
        P("dp", "seq", None),
        P("dp", "seq", None),
        P("dp", "seq", None),
        P(),
        P("dp", "seq", None),
        P("dp", None),
    )
    out_specs = (P("dp", "seq", None), P("dp", "seq", None), P("dp", "seq", None), P("seq", None))
    by_heads = mesh.shape["seq"] == 8 and mesh.shape["dp"] & (mesh.shape["dp"] - 1) == 0
    body = head_body if by_heads else halo_body
    return jax.shard_map(body, mesh=mesh, in_specs=in_specs, out_specs=out_specs, check_vma=False)
```

```python
import functools
import math

import jax
import jax.numpy as jnp
from jax import lax
from jax.experimental import pallas as pl
from jax.experimental.pallas import tpu as pltpu
from jax.sharding import PartitionSpec as P

HEADS = 16
HEAD_DIM = 72
MAXLEN = 384


NEG_FILL = -1e30


def shifted(block, axis, distance):
    devices = range(lax.axis_size(axis))
    route = [(i - distance, i) for i in devices if i - distance in devices]
    return lax.ppermute(block, axis, route)


def split_heads(rows_in):
    return rows_in.reshape(rows_in.shape[0], HEADS, HEAD_DIM)


def image_ids(image_ends, shard, tok_rows, shards):
    positions = shard * tok_rows + jnp.arange(tok_rows, dtype=jnp.int32)
    found = jnp.sum((positions[:, None] >= image_ends[None, :]).astype(jnp.int32), axis=1)
    inside = jnp.logical_and(shard >= 0, shard < shards)
    return jnp.where(inside, found, -1)


def masked_scores(q_rows, k_rows, q_ids, k_ids):
    scores = jnp.einsum(
        "qhd,khd->hqk", split_heads(q_rows), split_heads(k_rows), preferred_element_type=jnp.float32
    ) * HEAD_DIM ** (-0.5)
    same_image = q_ids[:, None] == k_ids[None, :]
    return jnp.where(same_image[None, :, :], scores, NEG_FILL)


def touches(q_ids, k_ids):
    return jnp.any(q_ids[:, None] == k_ids[None, :])


def make_probs(q_rows, k_rows, q_ids, k_ids, log_norm):
    return jnp.exp(masked_scores(q_rows, k_rows, q_ids, k_ids) - log_norm[:, :, None]).astype(
        jnp.bfloat16
    )


def score_grads(q_rows, k_rows, v_rows, d_rows, q_ids, k_ids, log_norm, row_delta):
    weights = make_probs(q_rows, k_rows, q_ids, k_ids, log_norm)
    d_probs = jnp.einsum(
        "qhd,khd->hqk", split_heads(d_rows), split_heads(v_rows), preferred_element_type=jnp.float32
    )
    d_scores = (
        HEAD_DIM ** (-0.5) * weights.astype(jnp.float32) * (d_probs - row_delta[:, :, None])
    ).astype(jnp.bfloat16)
    return (weights, d_scores)


def query_part(d_scores, k_rows):
    return jnp.einsum(
        "hqk,khd->qhd", d_scores, split_heads(k_rows), preferred_element_type=jnp.float32
    )


def key_part(weights, d_scores, q_rows, d_rows):
    k_part = jnp.einsum(
        "hqk,qhd->khd", d_scores, split_heads(q_rows), preferred_element_type=jnp.float32
    )
    v_part = jnp.einsum(
        "hqk,qhd->khd", weights, split_heads(d_rows), preferred_element_type=jnp.float32
    )
    return (k_part, v_part)


def halo_body(queries, keys, values, out_weight, out_grad, lengths):
    q_rows = queries[0]
    k_rows = keys[0]
    v_rows = values[0]
    dy_rows = out_grad[0]
    tok_rows = q_rows.shape[0]
    feature_width = q_rows.shape[1]
    shards = lax.axis_size("seq")
    seq_index = lax.axis_index("seq")
    key_reach = (MAXLEN + tok_rows - 2) // tok_rows
    image_ends = jnp.cumsum(lengths[0])
    own_ids = image_ids(image_ends, seq_index, tok_rows, shards)
    d_out = jnp.einsum("td,ed->te", dy_rows, out_weight, preferred_element_type=jnp.float32).astype(
        jnp.bfloat16
    )
    remote = []
    for distance in range(1, key_reach + 1):
        for offset in (distance, -distance):
            arrived = shifted((k_rows, v_rows), "seq", offset)
            remote.append((offset, arrived[0], arrived[1]))
    remote_ids = [image_ids(image_ends, seq_index - entry[0], tok_rows, shards) for entry in remote]
    own_scores = masked_scores(q_rows, k_rows, own_ids, own_ids)
    row_max = jnp.max(own_scores, axis=2)
    row_sum = jnp.sum(jnp.exp(own_scores - row_max[:, :, None]), axis=2)
    for entry, tile_ids in zip(remote, remote_ids):
        k_tile = entry[1]

        def widen(carried):
            old_max, old_sum = carried
            scores = masked_scores(q_rows, k_tile, own_ids, tile_ids)
            new_max = jnp.maximum(old_max, jnp.max(scores, axis=2))
            new_sum = old_sum * jnp.exp(old_max - new_max) + jnp.sum(
                jnp.exp(scores - new_max[:, :, None]), axis=2
            )
            return (new_max, new_sum)

        row_max, row_sum = lax.cond(
            touches(own_ids, tile_ids), widen, lambda carried: carried, (row_max, row_sum)
        )
    log_norm = row_max + jnp.log(row_sum)
    head_zeros = jnp.zeros((tok_rows, HEADS, HEAD_DIM), jnp.float32)
    mixed_sum = jnp.einsum(
        "hqk,khd->qhd",
        make_probs(q_rows, k_rows, own_ids, own_ids, log_norm),
        split_heads(v_rows),
        preferred_element_type=jnp.float32,
    )
    for entry, tile_ids in zip(remote, remote_ids):
        k_tile = entry[1]
        v_tile = entry[2]

        def mix_tile():
            weights = make_probs(q_rows, k_tile, own_ids, tile_ids, log_norm)
            return jnp.einsum(
                "hqk,khd->qhd", weights, split_heads(v_tile), preferred_element_type=jnp.float32
            )

        mixed_sum = mixed_sum + lax.cond(touches(own_ids, tile_ids), mix_tile, lambda: head_zeros)
    attended = mixed_sum.reshape(tok_rows, feature_width).astype(jnp.bfloat16)
    row_delta = jnp.sum(
        (d_out.astype(jnp.float32) * attended.astype(jnp.float32)).reshape(
            tok_rows, HEADS, HEAD_DIM
        ),
        axis=2,
    ).T
    weights, d_scores = score_grads(
        q_rows, k_rows, v_rows, d_out, own_ids, own_ids, log_norm, row_delta
    )
    q_grad = query_part(d_scores, k_rows)
    k_grad, v_grad = key_part(weights, d_scores, q_rows, d_out)
    for entry, tile_ids in zip(remote, remote_ids):
        offset = entry[0]
        k_tile = entry[1]
        v_tile = entry[2]

        def all_parts():
            tile_weights, tile_scores = score_grads(
                q_rows, k_tile, v_tile, d_out, own_ids, tile_ids, log_norm, row_delta
            )
            k_part, v_part = key_part(tile_weights, tile_scores, q_rows, d_out)
            return (query_part(tile_scores, k_tile), k_part, v_part)

        parts = lax.cond(
            touches(own_ids, tile_ids), all_parts, lambda: (head_zeros, head_zeros, head_zeros)
        )
        q_grad = q_grad + parts[0]
        returned = shifted(
            (parts[1].reshape(tok_rows, feature_width), parts[2].reshape(tok_rows, feature_width)),
            "seq",
            -offset,
        )
        k_grad = k_grad + returned[0].reshape(tok_rows, HEADS, HEAD_DIM)
        v_grad = v_grad + returned[1].reshape(tok_rows, HEADS, HEAD_DIM)
    weight_share = lax.psum_scatter(
        jnp.einsum("tr,tc->rc", attended, dy_rows, preferred_element_type=jnp.float32),
        "seq",
        scatter_dimension=0,
        tiled=True,
    )
    weight_sum = lax.psum(weight_share, "dp")
    all_tokens = tok_rows * shards * lax.axis_size("dp")
    weight_grad = weight_sum * (1.0 / math.sqrt(all_tokens))
    return (
        q_grad.reshape(1, tok_rows, feature_width),
        k_grad.reshape(1, tok_rows, feature_width),
        v_grad.reshape(1, tok_rows, feature_width),
        weight_grad,
    )


BF16, F32 = jnp.bfloat16, jnp.float32
ANY = pl.BlockSpec(memory_space=pl.ANY)
VMEM = pl.BlockSpec(memory_space=pltpu.VMEM)
HBM = pl.BlockSpec(memory_space=pltpu.HBM)
SMEM = pl.BlockSpec(memory_space=pltpu.SMEM)
DMA = pltpu.SemaphoreType.DMA
PARAMS = pltpu.CompilerParams(vmem_limit_bytes=16 * 1024 * 1024)
NT = ((1,), (1,))


def dot(a, b, contract=((1,), (0,))):
    return lax.dot_general(a, b, (contract, ((), ())), preferred_element_type=F32)


def spread_kernel(q_ref, k_ref, v_ref, out_ref, rows_s, turned_s, in_sem, out_sem):
    shards, height, _ = out_ref.shape
    part = height // 3
    loads = [pltpu.make_async_copy(ref, rows_s.at[i], in_sem.at[i]) for i, ref in enumerate((q_ref, k_ref, v_ref))]
    for load in loads:
        load.start()
    stores = []
    for i, load in enumerate(loads):
        load.wait()
        turned = rows_s[i].T
        for shard in range(shards):
            turned_s[i, shard] = turned[shard * part:(shard + 1) * part, :]
        store = pltpu.make_async_copy(turned_s.at[i], out_ref.at[:, pl.ds(i * part, part), :], out_sem.at[i])
        store.start()
        stores.append(store)
    for store in stores:
        store.wait()


def collect_kernel(*refs):
    blocks, (q_ref, k_ref, v_ref, turned_s, rows_s, out_sem) = refs[:-6], refs[-6:]
    part = blocks[0].shape[0] // 3
    me = lax.axis_index("seq")
    for n, block in enumerate(blocks):
        turned_s[me ^ BACK_ORDER[n]] = block[...]
    stores = []
    for i, ref in enumerate((q_ref, k_ref, v_ref)):
        whole = jnp.concatenate([turned_s[n, i * part:(i + 1) * part, :] for n in range(len(blocks))], axis=0)
        rows_s[i] = whole.astype(F32).T
        store = pltpu.make_async_copy(rows_s.at[i], ref, out_sem.at[i])
        store.start()
        stores.append(store)
    for store in stores:
        store.wait()


def window_sizes(tok, shards):
    return min(2, shards), min((MAXLEN + tok - 2) // tok + 1, shards)


def each_image(lengths, tok, shards, work):
    least, most = window_sizes(tok, shards)

    def one_image(image, start):
        end = start + lengths[0, image]
        low = start // tok
        count = jnp.maximum((end - 1) // tok - low + 1, least)
        first = jnp.minimum(low, shards - count)
        for size in range(least, most + 1):
            @pl.when(count == size)
            def _():
                work(image, size, first, start, end)
        return end

    lax.fori_loop(0, lengths.shape[1], one_image, jnp.int32(0))


def store_heads(ref, block, columns):
    heads, padded, _ = ref.shape
    filler = jnp.zeros((padded - HEAD_DIM, block.shape[1]), F32)
    for head in range(heads):
        rows = block[head * HEAD_DIM:(head + 1) * HEAD_DIM, :]
        ref[head, :, columns] = jnp.concatenate([rows, filler], axis=0).astype(BF16)


def joined(ref, turned=False):
    heads = [ref[head].T if turned else ref[head] for head in range(ref.shape[0])]
    return jnp.concatenate([block[0:HEAD_DIM, :] for block in heads], axis=0).astype(BF16)


def forward_kernel(early, len_ref, w_ref, in_ref, *refs):
    pieces = refs[:early]
    (qt_s, k_s, vt_s, att_s, probs_s, d_s, wg_s, w_s, len_s, q_s, v_s, kt_s, sum_s, dy_s, len_sem, w_sem, dy_sem) = refs[early:]
    shards, height, tok = in_ref.shape
    part = height // 3
    heads = k_s.shape[0]
    scale = HEAD_DIM ** (-0.5)

    load_len = pltpu.make_async_copy(len_ref, len_s, len_sem)
    load_len.start()
    load_w = load_w_rows(w_ref, w_s, w_sem)
    loads = load_rows(pieces, dy_s, dy_sem)
    sum_s[...] = jnp.zeros_like(sum_s)
    for shard in range(shards):
        columns = slice(shard * tok, (shard + 1) * tok)
        for i, ref in enumerate((q_s, k_s, v_s)):
            store_heads(ref, in_ref[shard, i * part:(i + 1) * part, :].astype(F32), columns)
    for head in range(heads):
        qt_s[head] = q_s[head].T
        kt_s[head] = k_s[head].T
        vt_s[head] = v_s[head].T
    load_len.wait()

    def work(image, count, first, start, end):
        width = count * tok
        base = pl.multiple_of(first * tok, tok)
        columns = pl.ds(base, width)
        key_pos = base + lax.broadcasted_iota(jnp.int32, (width, 1), 0)
        key_in = jnp.logical_and(key_pos >= start, key_pos < end)
        query_pos = base + lax.broadcasted_iota(jnp.int32, (1, width), 1)
        query_in = jnp.logical_and(query_pos >= start, query_pos < end)
        for head in range(heads):
            scores = jnp.where(key_in, dot(kt_s[head, columns, :], q_s[head, :, columns]), NEG_FILL)
            top = jnp.max(scores, axis=0, keepdims=True)
            grown = jnp.exp((scores - top) * scale)
            total = jnp.sum(grown, axis=0, keepdims=True)
            probs = (grown * jnp.where(query_in, 1.0 / total, 0.0)).astype(BF16)
            probs_s[image, head, 0:width, 0:width] = probs
            sum_s[head, :, columns] += dot(v_s[head, :, columns], probs)

    each_image(len_s, tok, shards, work)
    att_s[...] = joined(sum_s)
    for n in range(early, shards):
        dy_s[piece_columns(n, tok), :] = jnp.zeros((tok, dy_s.shape[1]), BF16)
    load_w.wait()
    for load in loads:
        load.wait()
    for shard in range(0, shards, 2):
        d_block = dot(w_s[...], dy_s[shard * tok:(shard + 2) * tok, :], NT)
        store_heads(d_s, d_block, slice(shard * tok, (shard + 2) * tok))
    wg_s[...] = dot(att_s[...], dy_s[...])


def backward_kernel(early, len_ref, w_s, qt_s, k_s, vt_s, att_s, probs_s, d_ref, *refs):
    late = refs[:8 - early]
    outs = refs[8 - early:16 - early]
    (len_s, d_s, dt_s, dq_s, dk_s, dv_s, out_s, len_sem, out_sem) = refs[16 - early:]
    shards, height, tok = out_s.shape
    part = height // 3
    heads = d_s.shape[0]
    scale = HEAD_DIM ** (-0.5)
    load_len = pltpu.make_async_copy(len_ref, len_s, len_sem)
    load_len.start()
    d_s[...] = d_ref[...]
    for ref in (dq_s, dk_s, dv_s):
        ref[...] = jnp.zeros_like(ref)
    for n, piece in enumerate(late):
        store_heads(d_s, dot(w_s[...], piece[...], NT), piece_columns(early + n, tok))
    for head in range(heads):
        dt_s[head] = d_s[head].T
    load_len.wait()

    def work(image, count, first, start, end):
        width = count * tok
        columns = pl.ds(pl.multiple_of(first * tok, tok), width)
        att_all = att_s[:, columns].astype(F32)
        for head in range(heads):
            d = d_s[head, :, columns]
            probs = probs_s[image, head, 0:width, 0:width]
            att = att_all[head * HEAD_DIM:(head + 1) * HEAD_DIM, :]
            delta = jnp.sum(d[0:HEAD_DIM, :].astype(F32) * att, axis=0, keepdims=True)
            d_probs = dot(vt_s[head, columns, :], d)
            d_scores = (scale * probs.astype(F32) * (d_probs - delta)).astype(BF16)
            dq_s[head, :, columns] += dot(k_s[head, :, columns], d_scores)
            dk_s[head, columns, :] += dot(d_scores, qt_s[head, columns, :])
            dv_s[head, columns, :] += dot(probs, dt_s[head, columns, :])

    each_image(len_s, tok, shards, work)

    stores = []
    for i, ref in enumerate((dq_s, dk_s, dv_s)):
        whole = joined(ref, turned=i > 0)
        for shard in range(shards):
            out_s[shard, i * part:(i + 1) * part, :] = whole[:, shard * tok:(shard + 1) * tok]
    me = lax.axis_index("seq")
    for n in range(shards - 1, 0, -1):
        store = pltpu.make_async_copy(out_s.at[me ^ n], outs[n], out_sem.at[n])
        store.start()
        stores.append(store)
    outs[0][...] = out_s[me]
    for store in stores:
        store.wait()


def weight_kernel(early, att_ref, wg_ref, *refs):
    late, out_ref = refs[:-1], refs[-1]
    total = wg_ref[...]
    for n, piece in enumerate(late):
        total = total + dot(att_ref[:, piece_columns(early + n, piece.shape[0])], piece[...])
    out_ref[...] = total.astype(BF16)


def load_w_rows(w_ref, w_s, sem):
    part = w_s.shape[0]
    row = pl.multiple_of(lax.axis_index("seq") * part, part)
    load = pltpu.make_async_copy(w_ref.at[pl.ds(row, part), :], w_s, sem)
    load.start()
    return load


def piece_columns(n, tok):
    me = lax.axis_index("seq")
    owner = me ^ jnp.where(is_inner(me), INNER_SOURCES[n], OUTER_SOURCES[n])
    return pl.ds(pl.multiple_of(owner * tok, tok), tok)


def load_rows(pieces, dy_s, sems):
    loads = []
    for n, piece in enumerate(pieces):
        load = pltpu.make_async_copy(piece, dy_s.at[piece_columns(n, piece.shape[0]), :], sems.at[n])
        load.start()
        loads.append(load)
    return loads


BACK_ORDER = (0, 5, 3, 4, 2, 7, 6, 1)
FIFTH_PARTS = 4
INNER_SOURCES = (0, 2, 6, 4, 3, 1, 7, 5)
OUTER_SOURCES = (0, 2, 1, 3, 4, 6, 5, 7)


def is_inner(index):
    z = index // 2
    return jnp.logical_or(z == 1, z == 2)


def gather_steps(block, event):
    devices = range(8)
    along = [(i, i ^ 2) for i in devices]
    across = [(i, i ^ 1) for i in devices]
    middle = [(i, i ^ 6 if i // 2 in (1, 2) else i ^ 1) for i in devices]
    inner = is_inner(lax.axis_index("seq"))

    def move(value, pairs):
        return lax.ppermute(value, "seq", pairs)

    one = move(block, along)
    two = move(block, middle)
    one, two = after(one, event), after(two, event)
    three = move(one, middle)
    four = move(two, along)
    rows = block.shape[0] // FIFTH_PARTS
    five = jnp.concatenate([move(three[n * rows:(n + 1) * rows], along) for n in range(FIFTH_PARTS)])
    six = move(jnp.where(inner, two, four), across)
    seven = move(jnp.where(inner, three, five), across)
    return (block, one, two, three, four, five, six, seven)


def after(value, *events):
    return lax.optimization_barrier((value, *events))[0]


def in_hbm(*arrays):
    return [pltpu.with_memory_space_constraint(array, pltpu.HBM) for array in arrays]


def head_body(queries, keys, values, out_weight, out_grad, lengths):
    tok, width = queries.shape[1:]
    shards = lax.axis_size("seq")
    groups = lax.axis_size("dp")
    part = width // shards
    heads = HEADS // shards
    tokens = tok * shards
    padded = -(-HEAD_DIM // 16) * 16

    def shape(dims, kind=BF16):
        return jax.ShapeDtypeStruct(dims, kind)

    sent = pl.pallas_call(
        spread_kernel, out_shape=pltpu.HBM((shards, 3 * part, tok), BF16),
        in_specs=[HBM] * 3, out_specs=HBM, compiler_params=PARAMS,
        scratch_shapes=[pltpu.VMEM((3, tok, width), BF16), pltpu.VMEM((3, shards, part, tok), BF16), DMA((3,)), DMA((3,))],
    )(*in_hbm(queries[0], keys[0], values[0]))
    pieces = gather_steps(out_grad[0], sent)
    arrived = lax.all_to_all(after(sent, *pieces[1:3]), "seq", 0, 0, tiled=True)

    images = lengths.shape[1]
    window = window_sizes(tok, shards)[1] * tok
    wide, tall = (heads, padded, tokens), (heads, tokens, padded)
    flat, chance = (part, tokens), (images, heads, window, window)

    def scratch(*dims, kind=BF16):
        return [pltpu.VMEM(d, kind) for d in dims]

    len_s = pltpu.SMEM((1, images), jnp.int32)
    early = 6
    late = len(pieces) - early
    q_r, k_t, v_r, attended, probs, d_part, w_early, w_rows = pl.pallas_call(
        functools.partial(forward_kernel, early),
        out_shape=[shape(tall), shape(wide), shape(tall), shape(flat), shape(chance), shape(wide), shape((part, width), F32), shape((part, width))],
        in_specs=[HBM, HBM, VMEM] + [HBM] * early, out_specs=[VMEM] * 8, compiler_params=PARAMS,
        scratch_shapes=[len_s] + scratch(wide, wide, tall) + scratch(wide, kind=F32) + scratch((tokens, width))
        + [DMA, DMA, DMA((early,))],
    )(*in_hbm(lengths, out_weight), arrived, *in_hbm(*pieces[:early]))
    w_part = pl.pallas_call(
        functools.partial(weight_kernel, early), out_shape=shape((part, width)),
        in_specs=[VMEM] * (2 + late), out_specs=VMEM, compiler_params=PARAMS,
    )(attended, w_early, *pieces[early:])
    grads = pl.pallas_call(
        functools.partial(backward_kernel, early),
        out_shape=[shape((3 * part, tok))] + [pltpu.HBM((3 * part, tok), BF16)] * (shards - 1),
        in_specs=[HBM] + [VMEM] * (7 + late), out_specs=[VMEM] + [HBM] * (shards - 1), compiler_params=PARAMS,
        scratch_shapes=[len_s] + scratch(wide, tall) + scratch(wide, tall, tall, kind=F32)
        + scratch((shards, 3 * part, tok)) + [DMA, DMA((shards,))],
    )(*in_hbm(lengths), w_rows, q_r, k_t, v_r, attended, probs, d_part, *pieces[early:])
    sums = w_part.astype(F32)
    step = 1
    while step < groups:
        pairs = [(i, i ^ step) for i in range(groups)]
        sums = w_part.astype(F32) + after(lax.ppermute(w_part, "dp", pairs), grads[0]).astype(F32)
        w_part = lax.reduce_precision(sums, 8, 7).astype(BF16)
        step *= 2
    weight_grad = sums * (1.0 / math.sqrt(tokens * groups))

    returned = [grads[0]]
    for n in BACK_ORDER[1:]:
        block = after(grads[n], weight_grad) if n == BACK_ORDER[-1] else grads[n]
        returned.append(lax.ppermute(block, "seq", [(i, i ^ n) for i in range(shards)]))

    q_grad, k_grad, v_grad = pl.pallas_call(
        collect_kernel, out_shape=[shape((tok, width), F32)] * 3, in_specs=[VMEM] * shards, out_specs=[ANY] * 3,
        compiler_params=PARAMS,
        scratch_shapes=scratch((shards, 3 * part, tok)) + scratch((3, tok, width), kind=F32) + [DMA((3,))],
    )(*returned)
    return q_grad[None], k_grad[None], v_grad[None], weight_grad


def solution(mesh):
    in_specs = (
        P("dp", "seq", None),
        P("dp", "seq", None),
        P("dp", "seq", None),
        P(),
        P("dp", "seq", None),
        P("dp", None),
    )
    out_specs = (P("dp", "seq", None), P("dp", "seq", None), P("dp", "seq", None), P("seq", None))
    by_heads = mesh.shape["seq"] == 8 and mesh.shape["dp"] & (mesh.shape["dp"] - 1) == 0
    body = head_body if by_heads else halo_body
    return jax.shard_map(body, mesh=mesh, in_specs=in_specs, out_specs=out_specs, check_vma=False)
```

```python
import functools
import math

import jax
import jax.numpy as jnp
from jax import lax
from jax.experimental import pallas as pl
from jax.experimental.pallas import tpu as pltpu
from jax.sharding import PartitionSpec as P

HEADS = 16
HEAD_DIM = 72
MAXLEN = 384


NEG_FILL = -1e30


def shifted(block, axis, distance):
    devices = range(lax.axis_size(axis))
    route = [(i - distance, i) for i in devices if i - distance in devices]
    return lax.ppermute(block, axis, route)


def split_heads(rows_in):
    return rows_in.reshape(rows_in.shape[0], HEADS, HEAD_DIM)


def image_ids(image_ends, shard, tok_rows, shards):
    positions = shard * tok_rows + jnp.arange(tok_rows, dtype=jnp.int32)
    found = jnp.sum((positions[:, None] >= image_ends[None, :]).astype(jnp.int32), axis=1)
    inside = jnp.logical_and(shard >= 0, shard < shards)
    return jnp.where(inside, found, -1)


def masked_scores(q_rows, k_rows, q_ids, k_ids):
    scores = jnp.einsum(
        "qhd,khd->hqk", split_heads(q_rows), split_heads(k_rows), preferred_element_type=jnp.float32
    ) * HEAD_DIM ** (-0.5)
    same_image = q_ids[:, None] == k_ids[None, :]
    return jnp.where(same_image[None, :, :], scores, NEG_FILL)


def touches(q_ids, k_ids):
    return jnp.any(q_ids[:, None] == k_ids[None, :])


def make_probs(q_rows, k_rows, q_ids, k_ids, log_norm):
    return jnp.exp(masked_scores(q_rows, k_rows, q_ids, k_ids) - log_norm[:, :, None]).astype(
        jnp.bfloat16
    )


def score_grads(q_rows, k_rows, v_rows, d_rows, q_ids, k_ids, log_norm, row_delta):
    weights = make_probs(q_rows, k_rows, q_ids, k_ids, log_norm)
    d_probs = jnp.einsum(
        "qhd,khd->hqk", split_heads(d_rows), split_heads(v_rows), preferred_element_type=jnp.float32
    )
    d_scores = (
        HEAD_DIM ** (-0.5) * weights.astype(jnp.float32) * (d_probs - row_delta[:, :, None])
    ).astype(jnp.bfloat16)
    return (weights, d_scores)


def query_part(d_scores, k_rows):
    return jnp.einsum(
        "hqk,khd->qhd", d_scores, split_heads(k_rows), preferred_element_type=jnp.float32
    )


def key_part(weights, d_scores, q_rows, d_rows):
    k_part = jnp.einsum(
        "hqk,qhd->khd", d_scores, split_heads(q_rows), preferred_element_type=jnp.float32
    )
    v_part = jnp.einsum(
        "hqk,qhd->khd", weights, split_heads(d_rows), preferred_element_type=jnp.float32
    )
    return (k_part, v_part)


def halo_body(queries, keys, values, out_weight, out_grad, lengths):
    q_rows = queries[0]
    k_rows = keys[0]
    v_rows = values[0]
    dy_rows = out_grad[0]
    tok_rows = q_rows.shape[0]
    feature_width = q_rows.shape[1]
    shards = lax.axis_size("seq")
    seq_index = lax.axis_index("seq")
    key_reach = (MAXLEN + tok_rows - 2) // tok_rows
    image_ends = jnp.cumsum(lengths[0])
    own_ids = image_ids(image_ends, seq_index, tok_rows, shards)
    d_out = jnp.einsum("td,ed->te", dy_rows, out_weight, preferred_element_type=jnp.float32).astype(
        jnp.bfloat16
    )
    remote = []
    for distance in range(1, key_reach + 1):
        for offset in (distance, -distance):
            arrived = shifted((k_rows, v_rows), "seq", offset)
            remote.append((offset, arrived[0], arrived[1]))
    remote_ids = [image_ids(image_ends, seq_index - entry[0], tok_rows, shards) for entry in remote]
    own_scores = masked_scores(q_rows, k_rows, own_ids, own_ids)
    row_max = jnp.max(own_scores, axis=2)
    row_sum = jnp.sum(jnp.exp(own_scores - row_max[:, :, None]), axis=2)
    for entry, tile_ids in zip(remote, remote_ids):
        k_tile = entry[1]

        def widen(carried):
            old_max, old_sum = carried
            scores = masked_scores(q_rows, k_tile, own_ids, tile_ids)
            new_max = jnp.maximum(old_max, jnp.max(scores, axis=2))
            new_sum = old_sum * jnp.exp(old_max - new_max) + jnp.sum(
                jnp.exp(scores - new_max[:, :, None]), axis=2
            )
            return (new_max, new_sum)

        row_max, row_sum = lax.cond(
            touches(own_ids, tile_ids), widen, lambda carried: carried, (row_max, row_sum)
        )
    log_norm = row_max + jnp.log(row_sum)
    head_zeros = jnp.zeros((tok_rows, HEADS, HEAD_DIM), jnp.float32)
    mixed_sum = jnp.einsum(
        "hqk,khd->qhd",
        make_probs(q_rows, k_rows, own_ids, own_ids, log_norm),
        split_heads(v_rows),
        preferred_element_type=jnp.float32,
    )
    for entry, tile_ids in zip(remote, remote_ids):
        k_tile = entry[1]
        v_tile = entry[2]

        def mix_tile():
            weights = make_probs(q_rows, k_tile, own_ids, tile_ids, log_norm)
            return jnp.einsum(
                "hqk,khd->qhd", weights, split_heads(v_tile), preferred_element_type=jnp.float32
            )

        mixed_sum = mixed_sum + lax.cond(touches(own_ids, tile_ids), mix_tile, lambda: head_zeros)
    attended = mixed_sum.reshape(tok_rows, feature_width).astype(jnp.bfloat16)
    row_delta = jnp.sum(
        (d_out.astype(jnp.float32) * attended.astype(jnp.float32)).reshape(
            tok_rows, HEADS, HEAD_DIM
        ),
        axis=2,
    ).T
    weights, d_scores = score_grads(
        q_rows, k_rows, v_rows, d_out, own_ids, own_ids, log_norm, row_delta
    )
    q_grad = query_part(d_scores, k_rows)
    k_grad, v_grad = key_part(weights, d_scores, q_rows, d_out)
    for entry, tile_ids in zip(remote, remote_ids):
        offset = entry[0]
        k_tile = entry[1]
        v_tile = entry[2]

        def all_parts():
            tile_weights, tile_scores = score_grads(
                q_rows, k_tile, v_tile, d_out, own_ids, tile_ids, log_norm, row_delta
            )
            k_part, v_part = key_part(tile_weights, tile_scores, q_rows, d_out)
            return (query_part(tile_scores, k_tile), k_part, v_part)

        parts = lax.cond(
            touches(own_ids, tile_ids), all_parts, lambda: (head_zeros, head_zeros, head_zeros)
        )
        q_grad = q_grad + parts[0]
        returned = shifted(
            (parts[1].reshape(tok_rows, feature_width), parts[2].reshape(tok_rows, feature_width)),
            "seq",
            -offset,
        )
        k_grad = k_grad + returned[0].reshape(tok_rows, HEADS, HEAD_DIM)
        v_grad = v_grad + returned[1].reshape(tok_rows, HEADS, HEAD_DIM)
    weight_share = lax.psum_scatter(
        jnp.einsum("tr,tc->rc", attended, dy_rows, preferred_element_type=jnp.float32),
        "seq",
        scatter_dimension=0,
        tiled=True,
    )
    weight_sum = lax.psum(weight_share, "dp")
    all_tokens = tok_rows * shards * lax.axis_size("dp")
    weight_grad = weight_sum * (1.0 / math.sqrt(all_tokens))
    return (
        q_grad.reshape(1, tok_rows, feature_width),
        k_grad.reshape(1, tok_rows, feature_width),
        v_grad.reshape(1, tok_rows, feature_width),
        weight_grad,
    )


BF16, F32 = jnp.bfloat16, jnp.float32
ANY = pl.BlockSpec(memory_space=pl.ANY)
VMEM = pl.BlockSpec(memory_space=pltpu.VMEM)
HBM = pl.BlockSpec(memory_space=pltpu.HBM)
SMEM = pl.BlockSpec(memory_space=pltpu.SMEM)
DMA = pltpu.SemaphoreType.DMA
PARAMS = pltpu.CompilerParams(vmem_limit_bytes=16 * 1024 * 1024)
NT = ((1,), (1,))


def dot(a, b, contract=((1,), (0,))):
    return lax.dot_general(a, b, (contract, ((), ())), preferred_element_type=F32)


def spread_kernel(q_ref, k_ref, v_ref, out_ref, rows_s, turned_s, in_sem, out_sem):
    shards, height, _ = out_ref.shape
    part = height // 3
    loads = [pltpu.make_async_copy(ref, rows_s.at[i], in_sem.at[i]) for i, ref in enumerate((q_ref, k_ref, v_ref))]
    for load in loads:
        load.start()
    stores = []
    for i, load in enumerate(loads):
        load.wait()
        turned = rows_s[i].T
        for shard in range(shards):
            turned_s[i, shard] = turned[shard * part:(shard + 1) * part, :]
        store = pltpu.make_async_copy(turned_s.at[i], out_ref.at[:, pl.ds(i * part, part), :], out_sem.at[i])
        store.start()
        stores.append(store)
    for store in stores:
        store.wait()


def collect_kernel(*refs):
    blocks, (q_ref, k_ref, v_ref, turned_s, rows_s, out_sem) = refs[:-6], refs[-6:]
    part = blocks[0].shape[0] // 3
    me = lax.axis_index("seq")
    for n, block in enumerate(blocks):
        turned_s[me ^ BACK_ORDER[n]] = block[...]
    stores = []
    for i, ref in enumerate((q_ref, k_ref, v_ref)):
        whole = jnp.concatenate([turned_s[n, i * part:(i + 1) * part, :] for n in range(len(blocks))], axis=0)
        rows_s[i] = whole.astype(F32).T
        store = pltpu.make_async_copy(rows_s.at[i], ref, out_sem.at[i])
        store.start()
        stores.append(store)
    for store in stores:
        store.wait()


def window_sizes(tok, shards):
    return min(2, shards), min((MAXLEN + tok - 2) // tok + 1, shards)


def each_image(lengths, tok, shards, work):
    least, most = window_sizes(tok, shards)

    def one_image(image, start):
        end = start + lengths[0, image]
        low = start // tok
        count = jnp.maximum((end - 1) // tok - low + 1, least)
        first = jnp.minimum(low, shards - count)
        for size in range(least, most + 1):
            @pl.when(count == size)
            def _():
                work(image, size, first, start, end)
        return end

    lax.fori_loop(0, lengths.shape[1], one_image, jnp.int32(0))


def store_heads(ref, block, columns):
    heads, padded, _ = ref.shape
    filler = jnp.zeros((padded - HEAD_DIM, block.shape[1]), F32)
    for head in range(heads):
        rows = block[head * HEAD_DIM:(head + 1) * HEAD_DIM, :]
        ref[head, :, columns] = jnp.concatenate([rows, filler], axis=0).astype(BF16)


def joined(ref):
    return jnp.concatenate([ref[head, 0:HEAD_DIM, :] for head in range(ref.shape[0])], axis=0).astype(BF16)


def project_kernel(w_ref, *refs):
    pieces, (dy_s, d_s, w_s, w_sem, dy_sem) = refs[:-5], refs[-5:]
    load_w = load_w_rows(w_ref, w_s, w_sem)
    loads = load_rows(pieces, dy_s, dy_sem)
    load_w.wait()
    for load in loads:
        load.wait()
    step = 2 * pieces[0].shape[0]
    for start in range(0, dy_s.shape[0], step):
        columns = slice(start, start + step)
        store_heads(d_s, dot(w_s[...], dy_s[columns, :], NT), columns)


def forward_kernel(len_ref, in_ref, dy_ref, q_s, k_s, vt_s, att_s, probs_s, wg_s, len_s, v_s, kt_s, sum_s, len_sem):
    shards, height, tok = in_ref.shape
    part = height // 3
    heads = q_s.shape[0]
    scale = HEAD_DIM ** (-0.5)

    load_len = pltpu.make_async_copy(len_ref, len_s, len_sem)
    load_len.start()
    sum_s[...] = jnp.zeros_like(sum_s)
    for shard in range(shards):
        columns = slice(shard * tok, (shard + 1) * tok)
        for i, ref in enumerate((q_s, k_s, v_s)):
            store_heads(ref, in_ref[shard, i * part:(i + 1) * part, :].astype(F32), columns)
    for head in range(heads):
        kt_s[head] = k_s[head].T
        vt_s[head] = v_s[head].T
    load_len.wait()

    def work(image, count, first, start, end):
        width = count * tok
        base = pl.multiple_of(first * tok, tok)
        columns = pl.ds(base, width)
        key_pos = base + lax.broadcasted_iota(jnp.int32, (width, 1), 0)
        key_in = jnp.logical_and(key_pos >= start, key_pos < end)
        query_pos = base + lax.broadcasted_iota(jnp.int32, (1, width), 1)
        query_in = jnp.logical_and(query_pos >= start, query_pos < end)
        for head in range(heads):
            scores = jnp.where(key_in, dot(kt_s[head, columns, :], q_s[head, :, columns]), NEG_FILL)
            top = jnp.max(scores, axis=0, keepdims=True)
            grown = jnp.exp((scores - top) * scale)
            total = jnp.sum(grown, axis=0, keepdims=True)
            probs = (grown * jnp.where(query_in, 1.0 / total, 0.0)).astype(BF16)
            probs_s[image, head, 0:width, 0:width] = probs
            sum_s[head, :, columns] += dot(v_s[head, :, columns], probs)

    each_image(len_s, tok, shards, work)
    att_s[...] = joined(sum_s)
    wg_s[...] = dot(att_s[...], dy_ref[...]).astype(BF16)


def backward_kernel(len_ref, q_s, k_s, vt_s, att_s, probs_s, d_s, *refs):
    outs, (len_s, dq_s, dk_s, dv_s, out_s, len_sem, out_sem) = refs[:-7], refs[-7:]
    shards, height, tok = out_s.shape
    part = height // 3
    heads = d_s.shape[0]
    scale = HEAD_DIM ** (-0.5)
    load_len = pltpu.make_async_copy(len_ref, len_s, len_sem)
    load_len.start()
    for ref in (dq_s, dk_s, dv_s):
        ref[...] = jnp.zeros_like(ref)
    load_len.wait()

    def work(image, count, first, start, end):
        width = count * tok
        columns = pl.ds(pl.multiple_of(first * tok, tok), width)
        att_all = att_s[:, columns].astype(F32)
        for head in range(heads):
            d = d_s[head, :, columns]
            probs = probs_s[image, head, 0:width, 0:width]
            att = att_all[head * HEAD_DIM:(head + 1) * HEAD_DIM, :]
            delta = jnp.sum(d[0:HEAD_DIM, :].astype(F32) * att, axis=0, keepdims=True)
            d_probs = dot(vt_s[head, columns, :], d)
            d_scores = (scale * probs.astype(F32) * (d_probs - delta)).astype(BF16)
            dq_s[head, :, columns] += dot(k_s[head, :, columns], d_scores)
            dk_s[head, :, columns] += dot(q_s[head, :, columns], d_scores, NT)
            dv_s[head, :, columns] += dot(d, probs, NT)

    each_image(len_s, tok, shards, work)

    for i, ref in enumerate((dq_s, dk_s, dv_s)):
        whole = joined(ref)
        for shard in range(shards):
            out_s[shard, i * part:(i + 1) * part, :] = whole[:, shard * tok:(shard + 1) * tok]
    me = lax.axis_index("seq")
    stores = []
    for n in range(shards - 1, 0, -1):
        store = pltpu.make_async_copy(out_s.at[me ^ n], outs[n], out_sem.at[n])
        store.start()
        stores.append(store)
    outs[0][...] = out_s[me]
    for store in stores:
        store.wait()


def load_w_rows(w_ref, w_s, sem):
    part = w_s.shape[0]
    row = pl.multiple_of(lax.axis_index("seq") * part, part)
    load = pltpu.make_async_copy(w_ref.at[pl.ds(row, part), :], w_s, sem)
    load.start()
    return load


def piece_columns(n, tok):
    me = lax.axis_index("seq")
    owner = me ^ jnp.where(is_inner(me), INNER_SOURCES[n], OUTER_SOURCES[n])
    return pl.ds(pl.multiple_of(owner * tok, tok), tok)


def load_rows(pieces, dy_s, sems):
    loads = []
    for n, piece in enumerate(pieces):
        load = pltpu.make_async_copy(piece, dy_s.at[piece_columns(n, piece.shape[0]), :], sems.at[n])
        load.start()
        loads.append(load)
    return loads


BACK_ORDER = (0, 5, 3, 4, 7, 6, 2, 1)
PARTS = 2
INNER_SOURCES = (0, 2, 6, 4, 3, 1, 7, 5)
OUTER_SOURCES = (0, 2, 1, 3, 4, 6, 5, 7)


def is_inner(index):
    z = index // 2
    return jnp.logical_or(z == 1, z == 2)


def gather_steps(block, event):
    devices = range(8)
    along = [(i, i ^ 2) for i in devices]
    across = [(i, i ^ 1) for i in devices]
    middle = [(i, i ^ 6 if i // 2 in (1, 2) else i ^ 1) for i in devices]
    inner = is_inner(lax.axis_index("seq"))

    def move(value, pairs):
        return lax.ppermute(value, "seq", pairs)

    rows = block.shape[0] // PARTS
    one = [move(block[n * rows:(n + 1) * rows], along) for n in range(PARTS)]
    two = after(move(block, middle), event)
    three = [move(after(part, event), middle) for part in one]
    four = move(two, along)
    five = [move(part, along) for part in three]
    six = move(jnp.where(inner, two, four), across)
    seven = [move(jnp.where(inner, ready, came), across) for ready, came in zip(three, five)]
    whole = [jnp.concatenate(parts) for parts in (one, three, five, seven)]
    return (block, whole[0], two, whole[1], four, whole[2], six, whole[3]), three


def after(value, *events):
    return lax.optimization_barrier((value, *events))[0]


def in_hbm(*arrays):
    return [pltpu.with_memory_space_constraint(array, pltpu.HBM) for array in arrays]


def head_body(queries, keys, values, out_weight, out_grad, lengths):
    tok, width = queries.shape[1:]
    shards = lax.axis_size("seq")
    groups = lax.axis_size("dp")
    part = width // shards
    heads = HEADS // shards
    tokens = tok * shards
    padded = -(-HEAD_DIM // 16) * 16

    def shape(dims, kind=BF16):
        return jax.ShapeDtypeStruct(dims, kind)

    sent = pl.pallas_call(
        spread_kernel, out_shape=pltpu.HBM((shards, 3 * part, tok), BF16),
        in_specs=[HBM] * 3, out_specs=HBM, compiler_params=PARAMS,
        scratch_shapes=[pltpu.VMEM((3, tok, width), BF16), pltpu.VMEM((3, shards, part, tok), BF16), DMA((3,)), DMA((3,))],
    )(*in_hbm(queries[0], keys[0], values[0]))
    pieces, crossed = gather_steps(out_grad[0], sent)
    arrived = lax.all_to_all(after(sent, *crossed, pieces[4]), "seq", 0, 0, tiled=True)

    images = lengths.shape[1]
    window = window_sizes(tok, shards)[1] * tok
    wide, tall = (heads, padded, tokens), (heads, tokens, padded)
    flat, chance = (part, tokens), (images, heads, window, window)

    def scratch(*dims, kind=BF16):
        return [pltpu.VMEM(d, kind) for d in dims]

    len_s = pltpu.SMEM((1, images), jnp.int32)
    dy_all, d_heads = pl.pallas_call(
        project_kernel, out_shape=[shape((tokens, width)), shape(wide)],
        in_specs=[HBM] * (1 + len(pieces)), out_specs=[VMEM] * 2, compiler_params=PARAMS,
        scratch_shapes=scratch((part, width)) + [DMA, DMA((len(pieces),))],
    )(*in_hbm(out_weight, *pieces))
    *kept, w_part = pl.pallas_call(
        forward_kernel,
        out_shape=[shape(wide), shape(wide), shape(tall), shape(flat), shape(chance), shape((part, width))],
        in_specs=[HBM, VMEM, VMEM], out_specs=[VMEM] * 6, compiler_params=PARAMS,
        scratch_shapes=[len_s] + scratch(wide, tall) + scratch(wide, kind=F32) + [DMA],
    )(*in_hbm(lengths), arrived, dy_all)
    grads = pl.pallas_call(
        backward_kernel,
        out_shape=[shape((3 * part, tok))] + [pltpu.HBM((3 * part, tok), BF16)] * (shards - 1),
        in_specs=[HBM] + [VMEM] * 6, out_specs=[VMEM] + [HBM] * (shards - 1), compiler_params=PARAMS,
        scratch_shapes=[len_s] + scratch(wide, wide, wide, kind=F32)
        + scratch((shards, 3 * part, tok)) + [DMA, DMA((shards,))],
    )(*in_hbm(lengths), *kept, d_heads)
    sums = w_part.astype(F32)
    step = 1
    while step < groups:
        pairs = [(i, i ^ step) for i in range(groups)]
        sums = w_part.astype(F32) + after(lax.ppermute(w_part, "dp", pairs), grads[0]).astype(F32)
        w_part = lax.reduce_precision(sums, 8, 7).astype(BF16)
        step *= 2
    weight_grad = sums * (1.0 / math.sqrt(tokens * groups))

    returned = [grads[0]]
    for n in BACK_ORDER[1:]:
        block = after(grads[n], weight_grad) if n == BACK_ORDER[-1] else grads[n]
        returned.append(lax.ppermute(block, "seq", [(i, i ^ n) for i in range(shards)]))

    q_grad, k_grad, v_grad = pl.pallas_call(
        collect_kernel, out_shape=[shape((tok, width), F32)] * 3, in_specs=[VMEM] * shards, out_specs=[ANY] * 3,
        compiler_params=PARAMS,
        scratch_shapes=scratch((shards, 3 * part, tok)) + scratch((3, tok, width), kind=F32) + [DMA((3,))],
    )(*returned)
    return q_grad[None], k_grad[None], v_grad[None], weight_grad


def solution(mesh):
    in_specs = (
        P("dp", "seq", None),
        P("dp", "seq", None),
        P("dp", "seq", None),
        P(),
        P("dp", "seq", None),
        P("dp", None),
    )
    out_specs = (P("dp", "seq", None), P("dp", "seq", None), P("dp", "seq", None), P("seq", None))
    by_heads = mesh.shape["seq"] == 8 and mesh.shape["dp"] & (mesh.shape["dp"] - 1) == 0
    body = head_body if by_heads else halo_body
    return jax.shard_map(body, mesh=mesh, in_specs=in_specs, out_specs=out_specs, check_vma=False)
```

```python
import functools
import math

import jax
import jax.numpy as jnp
from jax import lax
from jax.experimental import pallas as pl
from jax.experimental.pallas import tpu as pltpu
from jax.sharding import PartitionSpec as P

HEADS = 16
HEAD_DIM = 72
MAXLEN = 384


NEG_FILL = -1e30


def shifted(block, axis, distance):
    devices = range(lax.axis_size(axis))
    route = [(i - distance, i) for i in devices if i - distance in devices]
    return lax.ppermute(block, axis, route)


def split_heads(rows_in):
    return rows_in.reshape(rows_in.shape[0], HEADS, HEAD_DIM)


def image_ids(image_ends, shard, tok_rows, shards):
    positions = shard * tok_rows + jnp.arange(tok_rows, dtype=jnp.int32)
    found = jnp.sum((positions[:, None] >= image_ends[None, :]).astype(jnp.int32), axis=1)
    inside = jnp.logical_and(shard >= 0, shard < shards)
    return jnp.where(inside, found, -1)


def masked_scores(q_rows, k_rows, q_ids, k_ids):
    scores = jnp.einsum(
        "qhd,khd->hqk", split_heads(q_rows), split_heads(k_rows), preferred_element_type=jnp.float32
    ) * HEAD_DIM ** (-0.5)
    same_image = q_ids[:, None] == k_ids[None, :]
    return jnp.where(same_image[None, :, :], scores, NEG_FILL)


def touches(q_ids, k_ids):
    return jnp.any(q_ids[:, None] == k_ids[None, :])


def make_probs(q_rows, k_rows, q_ids, k_ids, log_norm):
    return jnp.exp(masked_scores(q_rows, k_rows, q_ids, k_ids) - log_norm[:, :, None]).astype(
        jnp.bfloat16
    )


def score_grads(q_rows, k_rows, v_rows, d_rows, q_ids, k_ids, log_norm, row_delta):
    weights = make_probs(q_rows, k_rows, q_ids, k_ids, log_norm)
    d_probs = jnp.einsum(
        "qhd,khd->hqk", split_heads(d_rows), split_heads(v_rows), preferred_element_type=jnp.float32
    )
    d_scores = (
        HEAD_DIM ** (-0.5) * weights.astype(jnp.float32) * (d_probs - row_delta[:, :, None])
    ).astype(jnp.bfloat16)
    return (weights, d_scores)


def query_part(d_scores, k_rows):
    return jnp.einsum(
        "hqk,khd->qhd", d_scores, split_heads(k_rows), preferred_element_type=jnp.float32
    )


def key_part(weights, d_scores, q_rows, d_rows):
    k_part = jnp.einsum(
        "hqk,qhd->khd", d_scores, split_heads(q_rows), preferred_element_type=jnp.float32
    )
    v_part = jnp.einsum(
        "hqk,qhd->khd", weights, split_heads(d_rows), preferred_element_type=jnp.float32
    )
    return (k_part, v_part)


def halo_body(queries, keys, values, out_weight, out_grad, lengths):
    q_rows = queries[0]
    k_rows = keys[0]
    v_rows = values[0]
    dy_rows = out_grad[0]
    tok_rows = q_rows.shape[0]
    feature_width = q_rows.shape[1]
    shards = lax.axis_size("seq")
    seq_index = lax.axis_index("seq")
    key_reach = (MAXLEN + tok_rows - 2) // tok_rows
    image_ends = jnp.cumsum(lengths[0])
    own_ids = image_ids(image_ends, seq_index, tok_rows, shards)
    d_out = jnp.einsum("td,ed->te", dy_rows, out_weight, preferred_element_type=jnp.float32).astype(
        jnp.bfloat16
    )
    remote = []
    for distance in range(1, key_reach + 1):
        for offset in (distance, -distance):
            arrived = shifted((k_rows, v_rows), "seq", offset)
            remote.append((offset, arrived[0], arrived[1]))
    remote_ids = [image_ids(image_ends, seq_index - entry[0], tok_rows, shards) for entry in remote]
    own_scores = masked_scores(q_rows, k_rows, own_ids, own_ids)
    row_max = jnp.max(own_scores, axis=2)
    row_sum = jnp.sum(jnp.exp(own_scores - row_max[:, :, None]), axis=2)
    for entry, tile_ids in zip(remote, remote_ids):
        k_tile = entry[1]

        def widen(carried):
            old_max, old_sum = carried
            scores = masked_scores(q_rows, k_tile, own_ids, tile_ids)
            new_max = jnp.maximum(old_max, jnp.max(scores, axis=2))
            new_sum = old_sum * jnp.exp(old_max - new_max) + jnp.sum(
                jnp.exp(scores - new_max[:, :, None]), axis=2
            )
            return (new_max, new_sum)

        row_max, row_sum = lax.cond(
            touches(own_ids, tile_ids), widen, lambda carried: carried, (row_max, row_sum)
        )
    log_norm = row_max + jnp.log(row_sum)
    head_zeros = jnp.zeros((tok_rows, HEADS, HEAD_DIM), jnp.float32)
    mixed_sum = jnp.einsum(
        "hqk,khd->qhd",
        make_probs(q_rows, k_rows, own_ids, own_ids, log_norm),
        split_heads(v_rows),
        preferred_element_type=jnp.float32,
    )
    for entry, tile_ids in zip(remote, remote_ids):
        k_tile = entry[1]
        v_tile = entry[2]

        def mix_tile():
            weights = make_probs(q_rows, k_tile, own_ids, tile_ids, log_norm)
            return jnp.einsum(
                "hqk,khd->qhd", weights, split_heads(v_tile), preferred_element_type=jnp.float32
            )

        mixed_sum = mixed_sum + lax.cond(touches(own_ids, tile_ids), mix_tile, lambda: head_zeros)
    attended = mixed_sum.reshape(tok_rows, feature_width).astype(jnp.bfloat16)
    row_delta = jnp.sum(
        (d_out.astype(jnp.float32) * attended.astype(jnp.float32)).reshape(
            tok_rows, HEADS, HEAD_DIM
        ),
        axis=2,
    ).T
    weights, d_scores = score_grads(
        q_rows, k_rows, v_rows, d_out, own_ids, own_ids, log_norm, row_delta
    )
    q_grad = query_part(d_scores, k_rows)
    k_grad, v_grad = key_part(weights, d_scores, q_rows, d_out)
    for entry, tile_ids in zip(remote, remote_ids):
        offset = entry[0]
        k_tile = entry[1]
        v_tile = entry[2]

        def all_parts():
            tile_weights, tile_scores = score_grads(
                q_rows, k_tile, v_tile, d_out, own_ids, tile_ids, log_norm, row_delta
            )
            k_part, v_part = key_part(tile_weights, tile_scores, q_rows, d_out)
            return (query_part(tile_scores, k_tile), k_part, v_part)

        parts = lax.cond(
            touches(own_ids, tile_ids), all_parts, lambda: (head_zeros, head_zeros, head_zeros)
        )
        q_grad = q_grad + parts[0]
        returned = shifted(
            (parts[1].reshape(tok_rows, feature_width), parts[2].reshape(tok_rows, feature_width)),
            "seq",
            -offset,
        )
        k_grad = k_grad + returned[0].reshape(tok_rows, HEADS, HEAD_DIM)
        v_grad = v_grad + returned[1].reshape(tok_rows, HEADS, HEAD_DIM)
    weight_share = lax.psum_scatter(
        jnp.einsum("tr,tc->rc", attended, dy_rows, preferred_element_type=jnp.float32),
        "seq",
        scatter_dimension=0,
        tiled=True,
    )
    weight_sum = lax.psum(weight_share, "dp")
    all_tokens = tok_rows * shards * lax.axis_size("dp")
    weight_grad = weight_sum * (1.0 / math.sqrt(all_tokens))
    return (
        q_grad.reshape(1, tok_rows, feature_width),
        k_grad.reshape(1, tok_rows, feature_width),
        v_grad.reshape(1, tok_rows, feature_width),
        weight_grad,
    )


BF16, F32 = jnp.bfloat16, jnp.float32
ANY = pl.BlockSpec(memory_space=pl.ANY)
VMEM = pl.BlockSpec(memory_space=pltpu.VMEM)
HBM = pl.BlockSpec(memory_space=pltpu.HBM)
SMEM = pl.BlockSpec(memory_space=pltpu.SMEM)
DMA = pltpu.SemaphoreType.DMA
PARAMS = pltpu.CompilerParams(vmem_limit_bytes=16 * 1024 * 1024)
NT = ((1,), (1,))


def dot(a, b, contract=((1,), (0,))):
    return lax.dot_general(a, b, (contract, ((), ())), preferred_element_type=F32)


def spread_kernel(q_ref, k_ref, v_ref, out_ref, rows_s, turned_s, in_sem, out_sem):
    shards, height, _ = out_ref.shape
    part = height // 3
    loads = [pltpu.make_async_copy(ref, rows_s.at[i], in_sem.at[i]) for i, ref in enumerate((q_ref, k_ref, v_ref))]
    for load in loads:
        load.start()
    stores = []
    for i, load in enumerate(loads):
        load.wait()
        turned = rows_s[i].T
        for shard in range(shards):
            turned_s[i, shard] = turned[shard * part:(shard + 1) * part, :]
        store = pltpu.make_async_copy(turned_s.at[i], out_ref.at[:, pl.ds(i * part, part), :], out_sem.at[i])
        store.start()
        stores.append(store)
    for store in stores:
        store.wait()


def collect_kernel(*refs):
    blocks, (q_ref, k_ref, v_ref, turned_s, rows_s, out_sem) = refs[:-6], refs[-6:]
    part = blocks[0].shape[0] // 3
    me = lax.axis_index("seq")
    for n, block in enumerate(blocks):
        turned_s[me ^ BACK_ORDER[n]] = block[...]
    stores = []
    for i, ref in enumerate((q_ref, k_ref, v_ref)):
        whole = jnp.concatenate([turned_s[n, i * part:(i + 1) * part, :] for n in range(len(blocks))], axis=0)
        rows_s[i] = whole.astype(F32).T
        store = pltpu.make_async_copy(rows_s.at[i], ref, out_sem.at[i])
        store.start()
        stores.append(store)
    for store in stores:
        store.wait()


def window_sizes(tok, shards):
    return min(2, shards), min((MAXLEN + tok - 2) // tok + 1, shards)


def each_image(lengths, tok, shards, work):
    least, most = window_sizes(tok, shards)

    def one_image(image, start):
        end = start + lengths[0, image]
        low = start // tok
        count = jnp.maximum((end - 1) // tok - low + 1, least)
        first = jnp.minimum(low, shards - count)
        for size in range(least, most + 1):
            @pl.when(count == size)
            def _():
                work(image, size, first, start, end)
        return end

    lax.fori_loop(0, lengths.shape[1], one_image, jnp.int32(0))


def store_heads(ref, block, columns):
    heads, padded, _ = ref.shape
    filler = jnp.zeros((padded - HEAD_DIM, block.shape[1]), F32)
    for head in range(heads):
        rows = block[head * HEAD_DIM:(head + 1) * HEAD_DIM, :]
        ref[head, :, columns] = jnp.concatenate([rows, filler], axis=0).astype(BF16)


def joined(ref):
    return jnp.concatenate([ref[head, 0:HEAD_DIM, :] for head in range(ref.shape[0])], axis=0).astype(BF16)


def forward_kernel(early, len_ref, w_ref, in_ref, *refs):
    pieces = refs[:early]
    (q_s, k_s, vt_s, att_s, probs_s, d_s, wg_s, w_s, len_s, v_s, kt_s, sum_s, dy_s, len_sem, w_sem, dy_sem) = refs[early:]
    shards, height, tok = in_ref.shape
    part = height // 3
    heads = q_s.shape[0]
    scale = HEAD_DIM ** (-0.5)

    load_len = pltpu.make_async_copy(len_ref, len_s, len_sem)
    load_len.start()
    load_w = load_w_rows(w_ref, w_s, w_sem)
    loads = load_rows(pieces, dy_s, dy_sem)
    sum_s[...] = jnp.zeros_like(sum_s)
    for shard in range(shards):
        columns = slice(shard * tok, (shard + 1) * tok)
        for i, ref in enumerate((q_s, k_s, v_s)):
            store_heads(ref, in_ref[shard, i * part:(i + 1) * part, :].astype(F32), columns)
    for head in range(heads):
        kt_s[head] = k_s[head].T
        vt_s[head] = v_s[head].T
    load_len.wait()

    def work(image, count, first, start, end):
        width = count * tok
        base = pl.multiple_of(first * tok, tok)
        columns = pl.ds(base, width)
        key_pos = base + lax.broadcasted_iota(jnp.int32, (width, 1), 0)
        key_in = jnp.logical_and(key_pos >= start, key_pos < end)
        query_pos = base + lax.broadcasted_iota(jnp.int32, (1, width), 1)
        query_in = jnp.logical_and(query_pos >= start, query_pos < end)
        for head in range(heads):
            scores = jnp.where(key_in, dot(kt_s[head, columns, :], q_s[head, :, columns]), NEG_FILL)
            top = jnp.max(scores, axis=0, keepdims=True)
            grown = jnp.exp((scores - top) * scale)
            total = jnp.sum(grown, axis=0, keepdims=True)
            probs = (grown * jnp.where(query_in, 1.0 / total, 0.0)).astype(BF16)
            probs_s[image, head, 0:width, 0:width] = probs
            sum_s[head, :, columns] += dot(v_s[head, :, columns], probs)

    each_image(len_s, tok, shards, work)
    att_s[...] = joined(sum_s)
    for n in range(early, shards):
        dy_s[piece_columns(n, tok), :] = jnp.zeros((tok, dy_s.shape[1]), BF16)
    load_w.wait()
    for load in loads:
        load.wait()
    for shard in range(0, shards, 2):
        d_block = dot(w_s[...], dy_s[shard * tok:(shard + 2) * tok, :], NT)
        store_heads(d_s, d_block, slice(shard * tok, (shard + 2) * tok))
    wg_s[...] = dot(att_s[...], dy_s[...])


def backward_kernel(early, len_ref, w_s, q_s, k_s, vt_s, att_s, probs_s, d_ref, *refs):
    late = refs[:8 - early]
    outs = refs[8 - early:16 - early]
    (len_s, d_s, dq_s, dk_s, dv_s, out_s, len_sem, out_sem) = refs[16 - early:]
    shards, height, tok = out_s.shape
    part = height // 3
    heads = d_s.shape[0]
    scale = HEAD_DIM ** (-0.5)
    load_len = pltpu.make_async_copy(len_ref, len_s, len_sem)
    load_len.start()
    d_s[...] = d_ref[...]
    for ref in (dq_s, dk_s, dv_s):
        ref[...] = jnp.zeros_like(ref)
    for n, piece in enumerate(late):
        store_heads(d_s, dot(w_s[...], piece[...], NT), piece_columns(early + n, tok))
    load_len.wait()

    def work(image, count, first, start, end):
        width = count * tok
        columns = pl.ds(pl.multiple_of(first * tok, tok), width)
        att_all = att_s[:, columns].astype(F32)
        for head in range(heads):
            d = d_s[head, :, columns]
            probs = probs_s[image, head, 0:width, 0:width]
            att = att_all[head * HEAD_DIM:(head + 1) * HEAD_DIM, :]
            delta = jnp.sum(d.astype(F32)[0:HEAD_DIM, :] * att, axis=0, keepdims=True)
            d_probs = dot(vt_s[head, columns, :], d)
            d_scores = (scale * probs.astype(F32) * (d_probs - delta)).astype(BF16)
            dq_s[head, :, columns] += dot(k_s[head, :, columns], d_scores)
            dk_s[head, :, columns] += dot(q_s[head, :, columns], d_scores, NT)
            dv_s[head, :, columns] += dot(d, probs, NT)

    each_image(len_s, tok, shards, work)

    me = lax.axis_index("seq")
    stores = []
    for i, ref in enumerate((dq_s, dk_s, dv_s)):
        whole = joined(ref)
        rows = pl.ds(i * part, part)
        for shard in range(shards):
            out_s[shard, i * part:(i + 1) * part, :] = whole[:, shard * tok:(shard + 1) * tok]
        for n in BACK_ORDER[1:]:
            store = pltpu.make_async_copy(out_s.at[me ^ n, rows], outs[n].at[rows], out_sem.at[i, n])
            store.start()
            stores.append(store)
    outs[0][...] = out_s[me]
    for store in stores:
        store.wait()


def weight_kernel(early, att_ref, wg_ref, *refs):
    late, out_ref = refs[:-1], refs[-1]
    total = wg_ref[...]
    for n, piece in enumerate(late):
        total = total + dot(att_ref[:, piece_columns(early + n, piece.shape[0])], piece[...])
    out_ref[...] = total.astype(BF16)


def load_w_rows(w_ref, w_s, sem):
    part = w_s.shape[0]
    row = pl.multiple_of(lax.axis_index("seq") * part, part)
    load = pltpu.make_async_copy(w_ref.at[pl.ds(row, part), :], w_s, sem)
    load.start()
    return load


def piece_columns(n, tok):
    me = lax.axis_index("seq")
    owner = me ^ jnp.where(is_inner(me), INNER_SOURCES[n], OUTER_SOURCES[n])
    return pl.ds(pl.multiple_of(owner * tok, tok), tok)


def load_rows(pieces, dy_s, sems):
    loads = []
    for n, piece in enumerate(pieces):
        load = pltpu.make_async_copy(piece, dy_s.at[piece_columns(n, piece.shape[0]), :], sems.at[n])
        load.start()
        loads.append(load)
    return loads


BACK_ORDER = (0, 5, 3, 4, 7, 6, 2, 1)
FIFTH_PARTS = 4
INNER_SOURCES = (0, 2, 6, 4, 3, 1, 7, 5)
OUTER_SOURCES = (0, 2, 1, 3, 4, 6, 5, 7)


def is_inner(index):
    z = index // 2
    return jnp.logical_or(z == 1, z == 2)


def gather_steps(block, event):
    devices = range(8)
    along = [(i, i ^ 2) for i in devices]
    across = [(i, i ^ 1) for i in devices]
    middle = [(i, i ^ 6 if i // 2 in (1, 2) else i ^ 1) for i in devices]
    inner = is_inner(lax.axis_index("seq"))

    def move(value, pairs):
        return lax.ppermute(value, "seq", pairs)

    one = move(block, along)
    two = move(block, middle)
    one, two = after(one, event), after(two, event)
    three = move(one, middle)
    four = move(two, along)
    rows = block.shape[0] // FIFTH_PARTS
    five = jnp.concatenate([move(three[n * rows:(n + 1) * rows], along) for n in range(FIFTH_PARTS)])
    six = move(jnp.where(inner, two, four), across)
    seven = move(jnp.where(inner, three, five), across)
    return (block, one, two, three, four, five, six, seven)


def after(value, *events):
    return lax.optimization_barrier((value, *events))[0]


def in_hbm(*arrays):
    return [pltpu.with_memory_space_constraint(array, pltpu.HBM) for array in arrays]


def head_body(queries, keys, values, out_weight, out_grad, lengths):
    tok, width = queries.shape[1:]
    shards = lax.axis_size("seq")
    groups = lax.axis_size("dp")
    part = width // shards
    heads = HEADS // shards
    tokens = tok * shards
    padded = -(-HEAD_DIM // 16) * 16

    def shape(dims, kind=BF16):
        return jax.ShapeDtypeStruct(dims, kind)

    sent = pl.pallas_call(
        spread_kernel, out_shape=pltpu.HBM((shards, 3 * part, tok), BF16),
        in_specs=[HBM] * 3, out_specs=HBM, compiler_params=PARAMS,
        scratch_shapes=[pltpu.VMEM((3, tok, width), BF16), pltpu.VMEM((3, shards, part, tok), BF16), DMA((3,)), DMA((3,))],
    )(*in_hbm(queries[0], keys[0], values[0]))
    pieces = gather_steps(out_grad[0], sent)
    arrived = lax.all_to_all(after(sent, *pieces[1:3]), "seq", 0, 0, tiled=True)

    images = lengths.shape[1]
    window = window_sizes(tok, shards)[1] * tok
    wide, tall = (heads, padded, tokens), (heads, tokens, padded)
    flat, chance = (part, tokens), (images, heads, window, window)

    def scratch(*dims, kind=BF16):
        return [pltpu.VMEM(d, kind) for d in dims]

    len_s = pltpu.SMEM((1, images), jnp.int32)
    early = 6
    late = len(pieces) - early
    q_t, k_t, v_r, attended, probs, d_part, w_early, w_rows = pl.pallas_call(
        functools.partial(forward_kernel, early),
        out_shape=[shape(wide), shape(wide), shape(tall), shape(flat), shape(chance), shape(wide), shape((part, width), F32), shape((part, width))],
        in_specs=[HBM, HBM, VMEM] + [HBM] * early, out_specs=[VMEM] * 8, compiler_params=PARAMS,
        scratch_shapes=[len_s] + scratch(wide, tall) + scratch(wide, kind=F32) + scratch((tokens, width))
        + [DMA, DMA, DMA((early,))],
    )(*in_hbm(lengths, out_weight), arrived, *in_hbm(*pieces[:early]))
    w_part = pl.pallas_call(
        functools.partial(weight_kernel, early), out_shape=shape((part, width)),
        in_specs=[VMEM] * (2 + late), out_specs=VMEM, compiler_params=PARAMS,
    )(attended, w_early, *pieces[early:])
    grads = pl.pallas_call(
        functools.partial(backward_kernel, early),
        out_shape=[shape((3 * part, tok))] + [pltpu.HBM((3 * part, tok), BF16)] * (shards - 1),
        in_specs=[HBM] + [VMEM] * (7 + late), out_specs=[VMEM] + [HBM] * (shards - 1), compiler_params=PARAMS,
        scratch_shapes=[len_s] + scratch(wide) + scratch(wide, wide, wide, kind=F32)
        + scratch((shards, 3 * part, tok)) + [DMA, DMA((3, shards))],
    )(*in_hbm(lengths), w_rows, q_t, k_t, v_r, attended, probs, d_part, *pieces[early:])
    sums = w_part.astype(F32)
    step = 1
    while step < groups:
        pairs = [(i, i ^ step) for i in range(groups)]
        sums = w_part.astype(F32) + after(lax.ppermute(w_part, "dp", pairs), grads[0]).astype(F32)
        w_part = lax.reduce_precision(sums, 8, 7).astype(BF16)
        step *= 2
    weight_grad = sums * (1.0 / math.sqrt(tokens * groups))

    returned = [grads[0]]
    for n in BACK_ORDER[1:]:
        block = after(grads[n], weight_grad) if n == BACK_ORDER[-1] else grads[n]
        returned.append(lax.ppermute(block, "seq", [(i, i ^ n) for i in range(shards)]))

    q_grad, k_grad, v_grad = pl.pallas_call(
        collect_kernel, out_shape=[shape((tok, width), F32)] * 3, in_specs=[VMEM] * shards, out_specs=[ANY] * 3,
        compiler_params=PARAMS,
        scratch_shapes=scratch((shards, 3 * part, tok)) + scratch((3, tok, width), kind=F32) + [DMA((3,))],
    )(*returned)
    return q_grad[None], k_grad[None], v_grad[None], weight_grad


def solution(mesh):
    in_specs = (
        P("dp", "seq", None),
        P("dp", "seq", None),
        P("dp", "seq", None),
        P(),
        P("dp", "seq", None),
        P("dp", None),
    )
    out_specs = (P("dp", "seq", None), P("dp", "seq", None), P("dp", "seq", None), P("seq", None))
    by_heads = mesh.shape["seq"] == 8 and mesh.shape["dp"] & (mesh.shape["dp"] - 1) == 0
    body = head_body if by_heads else halo_body
    return jax.shard_map(body, mesh=mesh, in_specs=in_specs, out_specs=out_specs, check_vma=False)
```

```python
import functools
import math

import jax
import jax.numpy as jnp
from jax import lax
from jax.experimental import pallas as pl
from jax.experimental.pallas import tpu as pltpu
from jax.sharding import PartitionSpec as P

HEADS = 16
HEAD_DIM = 72
MAXLEN = 384


NEG_FILL = -1e30


def shifted(block, axis, distance):
    devices = range(lax.axis_size(axis))
    route = [(i - distance, i) for i in devices if i - distance in devices]
    return lax.ppermute(block, axis, route)


def split_heads(rows_in):
    return rows_in.reshape(rows_in.shape[0], HEADS, HEAD_DIM)


def image_ids(image_ends, shard, tok_rows, shards):
    positions = shard * tok_rows + jnp.arange(tok_rows, dtype=jnp.int32)
    found = jnp.sum((positions[:, None] >= image_ends[None, :]).astype(jnp.int32), axis=1)
    inside = jnp.logical_and(shard >= 0, shard < shards)
    return jnp.where(inside, found, -1)


def masked_scores(q_rows, k_rows, q_ids, k_ids):
    scores = jnp.einsum(
        "qhd,khd->hqk", split_heads(q_rows), split_heads(k_rows), preferred_element_type=jnp.float32
    ) * HEAD_DIM ** (-0.5)
    same_image = q_ids[:, None] == k_ids[None, :]
    return jnp.where(same_image[None, :, :], scores, NEG_FILL)


def touches(q_ids, k_ids):
    return jnp.any(q_ids[:, None] == k_ids[None, :])


def make_probs(q_rows, k_rows, q_ids, k_ids, log_norm):
    return jnp.exp(masked_scores(q_rows, k_rows, q_ids, k_ids) - log_norm[:, :, None]).astype(
        jnp.bfloat16
    )


def score_grads(q_rows, k_rows, v_rows, d_rows, q_ids, k_ids, log_norm, row_delta):
    weights = make_probs(q_rows, k_rows, q_ids, k_ids, log_norm)
    d_probs = jnp.einsum(
        "qhd,khd->hqk", split_heads(d_rows), split_heads(v_rows), preferred_element_type=jnp.float32
    )
    d_scores = (
        HEAD_DIM ** (-0.5) * weights.astype(jnp.float32) * (d_probs - row_delta[:, :, None])
    ).astype(jnp.bfloat16)
    return (weights, d_scores)


def query_part(d_scores, k_rows):
    return jnp.einsum(
        "hqk,khd->qhd", d_scores, split_heads(k_rows), preferred_element_type=jnp.float32
    )


def key_part(weights, d_scores, q_rows, d_rows):
    k_part = jnp.einsum(
        "hqk,qhd->khd", d_scores, split_heads(q_rows), preferred_element_type=jnp.float32
    )
    v_part = jnp.einsum(
        "hqk,qhd->khd", weights, split_heads(d_rows), preferred_element_type=jnp.float32
    )
    return (k_part, v_part)


def halo_body(queries, keys, values, out_weight, out_grad, lengths):
    q_rows = queries[0]
    k_rows = keys[0]
    v_rows = values[0]
    dy_rows = out_grad[0]
    tok_rows = q_rows.shape[0]
    feature_width = q_rows.shape[1]
    shards = lax.axis_size("seq")
    seq_index = lax.axis_index("seq")
    key_reach = (MAXLEN + tok_rows - 2) // tok_rows
    image_ends = jnp.cumsum(lengths[0])
    own_ids = image_ids(image_ends, seq_index, tok_rows, shards)
    d_out = jnp.einsum("td,ed->te", dy_rows, out_weight, preferred_element_type=jnp.float32).astype(
        jnp.bfloat16
    )
    remote = []
    for distance in range(1, key_reach + 1):
        for offset in (distance, -distance):
            arrived = shifted((k_rows, v_rows), "seq", offset)
            remote.append((offset, arrived[0], arrived[1]))
    remote_ids = [image_ids(image_ends, seq_index - entry[0], tok_rows, shards) for entry in remote]
    own_scores = masked_scores(q_rows, k_rows, own_ids, own_ids)
    row_max = jnp.max(own_scores, axis=2)
    row_sum = jnp.sum(jnp.exp(own_scores - row_max[:, :, None]), axis=2)
    for entry, tile_ids in zip(remote, remote_ids):
        k_tile = entry[1]

        def widen(carried):
            old_max, old_sum = carried
            scores = masked_scores(q_rows, k_tile, own_ids, tile_ids)
            new_max = jnp.maximum(old_max, jnp.max(scores, axis=2))
            new_sum = old_sum * jnp.exp(old_max - new_max) + jnp.sum(
                jnp.exp(scores - new_max[:, :, None]), axis=2
            )
            return (new_max, new_sum)

        row_max, row_sum = lax.cond(
            touches(own_ids, tile_ids), widen, lambda carried: carried, (row_max, row_sum)
        )
    log_norm = row_max + jnp.log(row_sum)
    head_zeros = jnp.zeros((tok_rows, HEADS, HEAD_DIM), jnp.float32)
    mixed_sum = jnp.einsum(
        "hqk,khd->qhd",
        make_probs(q_rows, k_rows, own_ids, own_ids, log_norm),
        split_heads(v_rows),
        preferred_element_type=jnp.float32,
    )
    for entry, tile_ids in zip(remote, remote_ids):
        k_tile = entry[1]
        v_tile = entry[2]

        def mix_tile():
            weights = make_probs(q_rows, k_tile, own_ids, tile_ids, log_norm)
            return jnp.einsum(
                "hqk,khd->qhd", weights, split_heads(v_tile), preferred_element_type=jnp.float32
            )

        mixed_sum = mixed_sum + lax.cond(touches(own_ids, tile_ids), mix_tile, lambda: head_zeros)
    attended = mixed_sum.reshape(tok_rows, feature_width).astype(jnp.bfloat16)
    row_delta = jnp.sum(
        (d_out.astype(jnp.float32) * attended.astype(jnp.float32)).reshape(
            tok_rows, HEADS, HEAD_DIM
        ),
        axis=2,
    ).T
    weights, d_scores = score_grads(
        q_rows, k_rows, v_rows, d_out, own_ids, own_ids, log_norm, row_delta
    )
    q_grad = query_part(d_scores, k_rows)
    k_grad, v_grad = key_part(weights, d_scores, q_rows, d_out)
    for entry, tile_ids in zip(remote, remote_ids):
        offset = entry[0]
        k_tile = entry[1]
        v_tile = entry[2]

        def all_parts():
            tile_weights, tile_scores = score_grads(
                q_rows, k_tile, v_tile, d_out, own_ids, tile_ids, log_norm, row_delta
            )
            k_part, v_part = key_part(tile_weights, tile_scores, q_rows, d_out)
            return (query_part(tile_scores, k_tile), k_part, v_part)

        parts = lax.cond(
            touches(own_ids, tile_ids), all_parts, lambda: (head_zeros, head_zeros, head_zeros)
        )
        q_grad = q_grad + parts[0]
        returned = shifted(
            (parts[1].reshape(tok_rows, feature_width), parts[2].reshape(tok_rows, feature_width)),
            "seq",
            -offset,
        )
        k_grad = k_grad + returned[0].reshape(tok_rows, HEADS, HEAD_DIM)
        v_grad = v_grad + returned[1].reshape(tok_rows, HEADS, HEAD_DIM)
    weight_share = lax.psum_scatter(
        jnp.einsum("tr,tc->rc", attended, dy_rows, preferred_element_type=jnp.float32),
        "seq",
        scatter_dimension=0,
        tiled=True,
    )
    weight_sum = lax.psum(weight_share, "dp")
    all_tokens = tok_rows * shards * lax.axis_size("dp")
    weight_grad = weight_sum * (1.0 / math.sqrt(all_tokens))
    return (
        q_grad.reshape(1, tok_rows, feature_width),
        k_grad.reshape(1, tok_rows, feature_width),
        v_grad.reshape(1, tok_rows, feature_width),
        weight_grad,
    )


BF16, F32 = jnp.bfloat16, jnp.float32
ANY = pl.BlockSpec(memory_space=pl.ANY)
VMEM = pl.BlockSpec(memory_space=pltpu.VMEM)
HBM = pl.BlockSpec(memory_space=pltpu.HBM)
SMEM = pl.BlockSpec(memory_space=pltpu.SMEM)
DMA = pltpu.SemaphoreType.DMA
PARAMS = pltpu.CompilerParams(vmem_limit_bytes=16 * 1024 * 1024)
NT = ((1,), (1,))


def dot(a, b, contract=((1,), (0,))):
    return lax.dot_general(a, b, (contract, ((), ())), preferred_element_type=F32)


def spread_kernel(q_ref, k_ref, v_ref, out_ref, rows_s, turned_s, in_sem, out_sem):
    shards, height, _ = out_ref.shape
    part = height // 3
    loads = [pltpu.make_async_copy(ref, rows_s.at[i], in_sem.at[i]) for i, ref in enumerate((q_ref, k_ref, v_ref))]
    for load in loads:
        load.start()
    stores = []
    for i, load in enumerate(loads):
        load.wait()
        turned = rows_s[i].T
        for shard in range(shards):
            turned_s[i, shard] = turned[shard * part:(shard + 1) * part, :]
        store = pltpu.make_async_copy(turned_s.at[i], out_ref.at[:, pl.ds(i * part, part), :], out_sem.at[i])
        store.start()
        stores.append(store)
    for store in stores:
        store.wait()


def collect_kernel(*refs):
    blocks, (q_ref, k_ref, v_ref, turned_s, rows_s, out_sem) = refs[:-6], refs[-6:]
    part = blocks[0].shape[0] // 3
    me = lax.axis_index("seq")
    for n, block in enumerate(blocks):
        turned_s[me ^ BACK_ORDER[n]] = block[...]
    stores = []
    for i, ref in enumerate((q_ref, k_ref, v_ref)):
        whole = jnp.concatenate([turned_s[n, i * part:(i + 1) * part, :] for n in range(len(blocks))], axis=0)
        rows_s[i] = whole.astype(F32).T
        store = pltpu.make_async_copy(rows_s.at[i], ref, out_sem.at[i])
        store.start()
        stores.append(store)
    for store in stores:
        store.wait()


def window_sizes(tok, shards):
    return min(2, shards), min((MAXLEN + tok - 2) // tok + 1, shards)


def each_image(lengths, tok, shards, work):
    least, most = window_sizes(tok, shards)

    def one_image(image, start):
        end = start + lengths[0, image]
        low = start // tok
        count = jnp.maximum((end - 1) // tok - low + 1, least)
        first = jnp.minimum(low, shards - count)
        for size in range(least, most + 1):
            @pl.when(count == size)
            def _():
                work(image, size, first, start, end)
        return end

    lax.fori_loop(0, lengths.shape[1], one_image, jnp.int32(0))


def store_heads(ref, block, columns):
    heads, padded, _ = ref.shape
    filler = jnp.zeros((padded - HEAD_DIM, block.shape[1]), F32)
    for head in range(heads):
        rows = block[head * HEAD_DIM:(head + 1) * HEAD_DIM, :]
        ref[head, :, columns] = jnp.concatenate([rows, filler], axis=0).astype(BF16)


def joined(ref):
    return jnp.concatenate([ref[head, 0:HEAD_DIM, :] for head in range(ref.shape[0])], axis=0).astype(BF16)


def forward_kernel(early, len_ref, w_ref, in_ref, *refs):
    pieces = refs[:early]
    (q_s, k_s, vt_s, att_s, probs_s, d_s, wg_s, w_s, len_s, v_s, kt_s, sum_s, dy_s, len_sem, w_sem, dy_sem) = refs[early:]
    shards, height, tok = in_ref.shape
    part = height // 3
    heads = q_s.shape[0]
    scale = HEAD_DIM ** (-0.5)

    load_len = pltpu.make_async_copy(len_ref, len_s, len_sem)
    load_len.start()
    load_w = load_w_rows(w_ref, w_s, w_sem)
    loads = load_rows(pieces, dy_s, dy_sem)
    sum_s[...] = jnp.zeros_like(sum_s)
    for shard in range(shards):
        columns = slice(shard * tok, (shard + 1) * tok)
        for i, ref in enumerate((q_s, k_s, v_s)):
            store_heads(ref, in_ref[shard, i * part:(i + 1) * part, :].astype(F32), columns)
    for head in range(heads):
        kt_s[head] = k_s[head].T
        vt_s[head] = v_s[head].T
    load_len.wait()

    def work(image, count, first, start, end):
        width = count * tok
        base = pl.multiple_of(first * tok, tok)
        columns = pl.ds(base, width)
        key_pos = base + lax.broadcasted_iota(jnp.int32, (width, 1), 0)
        key_in = jnp.logical_and(key_pos >= start, key_pos < end)
        query_pos = base + lax.broadcasted_iota(jnp.int32, (1, width), 1)
        query_in = jnp.logical_and(query_pos >= start, query_pos < end)
        for head in range(heads):
            scores = jnp.where(key_in, dot(kt_s[head, columns, :], q_s[head, :, columns]), NEG_FILL)
            top = jnp.max(scores, axis=0, keepdims=True)
            grown = jnp.exp((scores - top) * scale)
            total = jnp.sum(grown, axis=0, keepdims=True)
            probs = (grown * jnp.where(query_in, 1.0 / total, 0.0)).astype(BF16)
            probs_s[image, head, 0:width, 0:width] = probs
            sum_s[head, :, columns] += dot(v_s[head, :, columns], probs)

    each_image(len_s, tok, shards, work)
    att_s[...] = joined(sum_s)
    for n in range(early, shards):
        dy_s[piece_columns(n, tok), :] = jnp.zeros((tok, dy_s.shape[1]), BF16)
    load_w.wait()
    for load in loads:
        load.wait()
    for shard in range(0, shards, 2):
        d_block = dot(w_s[...], dy_s[shard * tok:(shard + 2) * tok, :], NT)
        store_heads(d_s, d_block, slice(shard * tok, (shard + 2) * tok))
    wg_s[...] = dot(att_s[...], dy_s[...])


def backward_kernel(early, len_ref, w_s, q_s, k_s, vt_s, att_s, probs_s, d_ref, *refs):
    late = refs[:8 - early]
    outs = refs[8 - early:16 - early]
    (len_s, d_s, dq_s, dk_s, dv_s, out_s, len_sem, out_sem) = refs[16 - early:]
    shards, height, tok = out_s.shape
    part = height // 3
    heads = d_s.shape[0]
    scale = HEAD_DIM ** (-0.5)
    load_len = pltpu.make_async_copy(len_ref, len_s, len_sem)
    load_len.start()
    d_s[...] = d_ref[...]
    for ref in (dq_s, dk_s, dv_s):
        ref[...] = jnp.zeros_like(ref)
    for n, piece in enumerate(late):
        store_heads(d_s, dot(w_s[...], piece[...], NT), piece_columns(early + n, tok))
    load_len.wait()

    def work(image, count, first, start, end):
        width = count * tok
        columns = pl.ds(pl.multiple_of(first * tok, tok), width)
        att_all = att_s[:, columns].astype(F32)
        for head in range(heads):
            d = d_s[head, :, columns]
            probs = probs_s[image, head, 0:width, 0:width]
            att = att_all[head * HEAD_DIM:(head + 1) * HEAD_DIM, :]
            delta = jnp.sum(d.astype(F32)[0:HEAD_DIM, :] * att, axis=0, keepdims=True)
            d_probs = dot(vt_s[head, columns, :], d)
            d_scores = (scale * probs.astype(F32) * (d_probs - delta)).astype(BF16)
            dq_s[head, :, columns] += dot(k_s[head, :, columns], d_scores)
            dk_s[head, :, columns] += dot(q_s[head, :, columns], d_scores, NT)
            dv_s[head, :, columns] += dot(d, probs, NT)

    each_image(len_s, tok, shards, work)

    me = lax.axis_index("seq")
    stores = []
    for i, ref in enumerate((dq_s, dk_s, dv_s)):
        whole = joined(ref)
        rows = pl.ds(i * part, part)
        for shard in range(shards):
            out_s[shard, i * part:(i + 1) * part, :] = whole[:, shard * tok:(shard + 1) * tok]
        for n in BACK_ORDER[1:]:
            store = pltpu.make_async_copy(out_s.at[me ^ n, rows], outs[n].at[rows], out_sem.at[i, n])
            store.start()
            stores.append(store)
    outs[0][...] = out_s[me]
    for store in stores:
        store.wait()


def weight_kernel(early, att_ref, wg_ref, *refs):
    late, out_ref = refs[:-1], refs[-1]
    total = wg_ref[...]
    for n, piece in enumerate(late):
        total = total + dot(att_ref[:, piece_columns(early + n, piece.shape[0])], piece[...])
    out_ref[...] = total.astype(BF16)


def load_w_rows(w_ref, w_s, sem):
    part = w_s.shape[0]
    row = pl.multiple_of(lax.axis_index("seq") * part, part)
    load = pltpu.make_async_copy(w_ref.at[pl.ds(row, part), :], w_s, sem)
    load.start()
    return load


def piece_columns(n, tok):
    me = lax.axis_index("seq")
    owner = me ^ jnp.where(is_inner(me), INNER_SOURCES[n], OUTER_SOURCES[n])
    return pl.ds(pl.multiple_of(owner * tok, tok), tok)


def load_rows(pieces, dy_s, sems):
    loads = []
    for n, piece in enumerate(pieces):
        load = pltpu.make_async_copy(piece, dy_s.at[piece_columns(n, piece.shape[0]), :], sems.at[n])
        load.start()
        loads.append(load)
    return loads


BACK_ORDER = (0, 5, 3, 4, 7, 2, 6, 1)
FIFTH_PARTS = 4
INNER_SOURCES = (0, 2, 6, 4, 3, 1, 7, 5)
OUTER_SOURCES = (0, 2, 1, 3, 4, 6, 5, 7)


def is_inner(index):
    z = index // 2
    return jnp.logical_or(z == 1, z == 2)


def gather_steps(block, event):
    devices = range(8)
    along = [(i, i ^ 2) for i in devices]
    across = [(i, i ^ 1) for i in devices]
    middle = [(i, i ^ 6 if i // 2 in (1, 2) else i ^ 1) for i in devices]
    inner = is_inner(lax.axis_index("seq"))

    def move(value, pairs):
        return lax.ppermute(value, "seq", pairs)

    one = move(block, along)
    two = move(block, middle)
    one, two = after(one, event), after(two, event)
    three = move(one, middle)
    four = move(two, along)
    rows = block.shape[0] // FIFTH_PARTS
    five = jnp.concatenate([move(three[n * rows:(n + 1) * rows], along) for n in range(FIFTH_PARTS)])
    six = move(jnp.where(inner, two, four), across)
    seven = move(jnp.where(inner, three, five), across)
    return (block, one, two, three, four, five, six, seven)


def after(value, *events):
    return lax.optimization_barrier((value, *events))[0]


def in_hbm(*arrays):
    return [pltpu.with_memory_space_constraint(array, pltpu.HBM) for array in arrays]


def head_body(queries, keys, values, out_weight, out_grad, lengths):
    tok, width = queries.shape[1:]
    shards = lax.axis_size("seq")
    groups = lax.axis_size("dp")
    part = width // shards
    heads = HEADS // shards
    tokens = tok * shards
    padded = -(-HEAD_DIM // 16) * 16

    def shape(dims, kind=BF16):
        return jax.ShapeDtypeStruct(dims, kind)

    sent = pl.pallas_call(
        spread_kernel, out_shape=pltpu.HBM((shards, 3 * part, tok), BF16),
        in_specs=[HBM] * 3, out_specs=HBM, compiler_params=PARAMS,
        scratch_shapes=[pltpu.VMEM((3, tok, width), BF16), pltpu.VMEM((3, shards, part, tok), BF16), DMA((3,)), DMA((3,))],
    )(*in_hbm(queries[0], keys[0], values[0]))
    pieces = gather_steps(out_grad[0], sent)
    arrived = lax.all_to_all(after(sent, *pieces[1:3]), "seq", 0, 0, tiled=True)

    images = lengths.shape[1]
    window = window_sizes(tok, shards)[1] * tok
    wide, tall = (heads, padded, tokens), (heads, tokens, padded)
    flat, chance = (part, tokens), (images, heads, window, window)

    def scratch(*dims, kind=BF16):
        return [pltpu.VMEM(d, kind) for d in dims]

    len_s = pltpu.SMEM((1, images), jnp.int32)
    early = 6
    late = len(pieces) - early
    q_t, k_t, v_r, attended, probs, d_part, w_early, w_rows = pl.pallas_call(
        functools.partial(forward_kernel, early),
        out_shape=[shape(wide), shape(wide), shape(tall), shape(flat), shape(chance), shape(wide), shape((part, width), F32), shape((part, width))],
        in_specs=[HBM, HBM, VMEM] + [HBM] * early, out_specs=[VMEM] * 8, compiler_params=PARAMS,
        scratch_shapes=[len_s] + scratch(wide, tall) + scratch(wide, kind=F32) + scratch((tokens, width))
        + [DMA, DMA, DMA((early,))],
    )(*in_hbm(lengths, out_weight), arrived, *in_hbm(*pieces[:early]))
    w_part = pl.pallas_call(
        functools.partial(weight_kernel, early), out_shape=shape((part, width)),
        in_specs=[VMEM] * (2 + late), out_specs=VMEM, compiler_params=PARAMS,
    )(attended, w_early, *pieces[early:])
    grads = pl.pallas_call(
        functools.partial(backward_kernel, early),
        out_shape=[shape((3 * part, tok))] + [pltpu.HBM((3 * part, tok), BF16)] * (shards - 1),
        in_specs=[HBM] + [VMEM] * (7 + late), out_specs=[VMEM] + [HBM] * (shards - 1), compiler_params=PARAMS,
        scratch_shapes=[len_s] + scratch(wide) + scratch(wide, wide, wide, kind=F32)
        + scratch((shards, 3 * part, tok)) + [DMA, DMA((3, shards))],
    )(*in_hbm(lengths), w_rows, q_t, k_t, v_r, attended, probs, d_part, *pieces[early:])
    sums = w_part.astype(F32)
    step = 1
    while step < groups:
        pairs = [(i, i ^ step) for i in range(groups)]
        sums = w_part.astype(F32) + after(lax.ppermute(w_part, "dp", pairs), grads[0]).astype(F32)
        w_part = lax.reduce_precision(sums, 8, 7).astype(BF16)
        step *= 2
    weight_grad = sums * (1.0 / math.sqrt(tokens * groups))

    returned = [grads[0]]
    for n in BACK_ORDER[1:]:
        block = after(grads[n], weight_grad) if n == BACK_ORDER[-1] else grads[n]
        returned.append(lax.ppermute(block, "seq", [(i, i ^ n) for i in range(shards)]))

    q_grad, k_grad, v_grad = pl.pallas_call(
        collect_kernel, out_shape=[shape((tok, width), F32)] * 3, in_specs=[VMEM] * shards, out_specs=[ANY] * 3,
        compiler_params=PARAMS,
        scratch_shapes=scratch((shards, 3 * part, tok)) + scratch((3, tok, width), kind=F32) + [DMA((3,))],
    )(*returned)
    return q_grad[None], k_grad[None], v_grad[None], weight_grad


def solution(mesh):
    in_specs = (
        P("dp", "seq", None),
        P("dp", "seq", None),
        P("dp", "seq", None),
        P(),
        P("dp", "seq", None),
        P("dp", None),
    )
    out_specs = (P("dp", "seq", None), P("dp", "seq", None), P("dp", "seq", None), P("seq", None))
    by_heads = mesh.shape["seq"] == 8 and mesh.shape["dp"] & (mesh.shape["dp"] - 1) == 0
    body = head_body if by_heads else halo_body
    return jax.shard_map(body, mesh=mesh, in_specs=in_specs, out_specs=out_specs, check_vma=False)
```

```python
import functools
import math

import jax
import jax.numpy as jnp
from jax import lax
from jax.experimental import pallas as pl
from jax.experimental.pallas import tpu as pltpu
from jax.sharding import PartitionSpec as P

HEADS = 16
HEAD_DIM = 72
MAXLEN = 384


NEG_FILL = -1e30


def shifted(block, axis, distance):
    devices = range(lax.axis_size(axis))
    route = [(i - distance, i) for i in devices if i - distance in devices]
    return lax.ppermute(block, axis, route)


def split_heads(rows_in):
    return rows_in.reshape(rows_in.shape[0], HEADS, HEAD_DIM)


def image_ids(image_ends, shard, tok_rows, shards):
    positions = shard * tok_rows + jnp.arange(tok_rows, dtype=jnp.int32)
    found = jnp.sum((positions[:, None] >= image_ends[None, :]).astype(jnp.int32), axis=1)
    inside = jnp.logical_and(shard >= 0, shard < shards)
    return jnp.where(inside, found, -1)


def masked_scores(q_rows, k_rows, q_ids, k_ids):
    scores = jnp.einsum(
        "qhd,khd->hqk", split_heads(q_rows), split_heads(k_rows), preferred_element_type=jnp.float32
    ) * HEAD_DIM ** (-0.5)
    same_image = q_ids[:, None] == k_ids[None, :]
    return jnp.where(same_image[None, :, :], scores, NEG_FILL)


def touches(q_ids, k_ids):
    return jnp.any(q_ids[:, None] == k_ids[None, :])


def make_probs(q_rows, k_rows, q_ids, k_ids, log_norm):
    return jnp.exp(masked_scores(q_rows, k_rows, q_ids, k_ids) - log_norm[:, :, None]).astype(
        jnp.bfloat16
    )


def score_grads(q_rows, k_rows, v_rows, d_rows, q_ids, k_ids, log_norm, row_delta):
    weights = make_probs(q_rows, k_rows, q_ids, k_ids, log_norm)
    d_probs = jnp.einsum(
        "qhd,khd->hqk", split_heads(d_rows), split_heads(v_rows), preferred_element_type=jnp.float32
    )
    d_scores = (
        HEAD_DIM ** (-0.5) * weights.astype(jnp.float32) * (d_probs - row_delta[:, :, None])
    ).astype(jnp.bfloat16)
    return (weights, d_scores)


def query_part(d_scores, k_rows):
    return jnp.einsum(
        "hqk,khd->qhd", d_scores, split_heads(k_rows), preferred_element_type=jnp.float32
    )


def key_part(weights, d_scores, q_rows, d_rows):
    k_part = jnp.einsum(
        "hqk,qhd->khd", d_scores, split_heads(q_rows), preferred_element_type=jnp.float32
    )
    v_part = jnp.einsum(
        "hqk,qhd->khd", weights, split_heads(d_rows), preferred_element_type=jnp.float32
    )
    return (k_part, v_part)


def halo_body(queries, keys, values, out_weight, out_grad, lengths):
    q_rows = queries[0]
    k_rows = keys[0]
    v_rows = values[0]
    dy_rows = out_grad[0]
    tok_rows = q_rows.shape[0]
    feature_width = q_rows.shape[1]
    shards = lax.axis_size("seq")
    seq_index = lax.axis_index("seq")
    key_reach = (MAXLEN + tok_rows - 2) // tok_rows
    image_ends = jnp.cumsum(lengths[0])
    own_ids = image_ids(image_ends, seq_index, tok_rows, shards)
    d_out = jnp.einsum("td,ed->te", dy_rows, out_weight, preferred_element_type=jnp.float32).astype(
        jnp.bfloat16
    )
    remote = []
    for distance in range(1, key_reach + 1):
        for offset in (distance, -distance):
            arrived = shifted((k_rows, v_rows), "seq", offset)
            remote.append((offset, arrived[0], arrived[1]))
    remote_ids = [image_ids(image_ends, seq_index - entry[0], tok_rows, shards) for entry in remote]
    own_scores = masked_scores(q_rows, k_rows, own_ids, own_ids)
    row_max = jnp.max(own_scores, axis=2)
    row_sum = jnp.sum(jnp.exp(own_scores - row_max[:, :, None]), axis=2)
    for entry, tile_ids in zip(remote, remote_ids):
        k_tile = entry[1]

        def widen(carried):
            old_max, old_sum = carried
            scores = masked_scores(q_rows, k_tile, own_ids, tile_ids)
            new_max = jnp.maximum(old_max, jnp.max(scores, axis=2))
            new_sum = old_sum * jnp.exp(old_max - new_max) + jnp.sum(
                jnp.exp(scores - new_max[:, :, None]), axis=2
            )
            return (new_max, new_sum)

        row_max, row_sum = lax.cond(
            touches(own_ids, tile_ids), widen, lambda carried: carried, (row_max, row_sum)
        )
    log_norm = row_max + jnp.log(row_sum)
    head_zeros = jnp.zeros((tok_rows, HEADS, HEAD_DIM), jnp.float32)
    mixed_sum = jnp.einsum(
        "hqk,khd->qhd",
        make_probs(q_rows, k_rows, own_ids, own_ids, log_norm),
        split_heads(v_rows),
        preferred_element_type=jnp.float32,
    )
    for entry, tile_ids in zip(remote, remote_ids):
        k_tile = entry[1]
        v_tile = entry[2]

        def mix_tile():
            weights = make_probs(q_rows, k_tile, own_ids, tile_ids, log_norm)
            return jnp.einsum(
                "hqk,khd->qhd", weights, split_heads(v_tile), preferred_element_type=jnp.float32
            )

        mixed_sum = mixed_sum + lax.cond(touches(own_ids, tile_ids), mix_tile, lambda: head_zeros)
    attended = mixed_sum.reshape(tok_rows, feature_width).astype(jnp.bfloat16)
    row_delta = jnp.sum(
        (d_out.astype(jnp.float32) * attended.astype(jnp.float32)).reshape(
            tok_rows, HEADS, HEAD_DIM
        ),
        axis=2,
    ).T
    weights, d_scores = score_grads(
        q_rows, k_rows, v_rows, d_out, own_ids, own_ids, log_norm, row_delta
    )
    q_grad = query_part(d_scores, k_rows)
    k_grad, v_grad = key_part(weights, d_scores, q_rows, d_out)
    for entry, tile_ids in zip(remote, remote_ids):
        offset = entry[0]
        k_tile = entry[1]
        v_tile = entry[2]

        def all_parts():
            tile_weights, tile_scores = score_grads(
                q_rows, k_tile, v_tile, d_out, own_ids, tile_ids, log_norm, row_delta
            )
            k_part, v_part = key_part(tile_weights, tile_scores, q_rows, d_out)
            return (query_part(tile_scores, k_tile), k_part, v_part)

        parts = lax.cond(
            touches(own_ids, tile_ids), all_parts, lambda: (head_zeros, head_zeros, head_zeros)
        )
        q_grad = q_grad + parts[0]
        returned = shifted(
            (parts[1].reshape(tok_rows, feature_width), parts[2].reshape(tok_rows, feature_width)),
            "seq",
            -offset,
        )
        k_grad = k_grad + returned[0].reshape(tok_rows, HEADS, HEAD_DIM)
        v_grad = v_grad + returned[1].reshape(tok_rows, HEADS, HEAD_DIM)
    weight_share = lax.psum_scatter(
        jnp.einsum("tr,tc->rc", attended, dy_rows, preferred_element_type=jnp.float32),
        "seq",
        scatter_dimension=0,
        tiled=True,
    )
    weight_sum = lax.psum(weight_share, "dp")
    all_tokens = tok_rows * shards * lax.axis_size("dp")
    weight_grad = weight_sum * (1.0 / math.sqrt(all_tokens))
    return (
        q_grad.reshape(1, tok_rows, feature_width),
        k_grad.reshape(1, tok_rows, feature_width),
        v_grad.reshape(1, tok_rows, feature_width),
        weight_grad,
    )


BF16, F32 = jnp.bfloat16, jnp.float32
ANY = pl.BlockSpec(memory_space=pl.ANY)
VMEM = pl.BlockSpec(memory_space=pltpu.VMEM)
HBM = pl.BlockSpec(memory_space=pltpu.HBM)
SMEM = pl.BlockSpec(memory_space=pltpu.SMEM)
DMA = pltpu.SemaphoreType.DMA
PARAMS = pltpu.CompilerParams(vmem_limit_bytes=16 * 1024 * 1024)
NT = ((1,), (1,))


def dot(a, b, contract=((1,), (0,))):
    return lax.dot_general(a, b, (contract, ((), ())), preferred_element_type=F32)


def spread_kernel(q_ref, k_ref, v_ref, out_ref, rows_s, turned_s, in_sem, out_sem):
    shards, height, _ = out_ref.shape
    part = height // 3
    loads = [pltpu.make_async_copy(ref, rows_s.at[i], in_sem.at[i]) for i, ref in enumerate((q_ref, k_ref, v_ref))]
    for load in loads:
        load.start()
    stores = []
    for i, load in enumerate(loads):
        load.wait()
        turned = rows_s[i].T
        for shard in range(shards):
            turned_s[i, shard] = turned[shard * part:(shard + 1) * part, :]
        store = pltpu.make_async_copy(turned_s.at[i], out_ref.at[:, pl.ds(i * part, part), :], out_sem.at[i])
        store.start()
        stores.append(store)
    for store in stores:
        store.wait()


def collect_kernel(*refs):
    blocks, (q_ref, k_ref, v_ref, turned_s, rows_s, out_sem) = refs[:-6], refs[-6:]
    part = blocks[0].shape[0] // 3
    me = lax.axis_index("seq")
    for n, block in enumerate(blocks):
        turned_s[me ^ BACK_ORDER[n]] = block[...]
    stores = []
    for i, ref in enumerate((q_ref, k_ref, v_ref)):
        whole = jnp.concatenate([turned_s[n, i * part:(i + 1) * part, :] for n in range(len(blocks))], axis=0)
        rows_s[i] = whole.astype(F32).T
        store = pltpu.make_async_copy(rows_s.at[i], ref, out_sem.at[i])
        store.start()
        stores.append(store)
    for store in stores:
        store.wait()


def window_sizes(tok, shards):
    return min(2, shards), min((MAXLEN + tok - 2) // tok + 1, shards)


def each_image(lengths, tok, shards, work):
    least, most = window_sizes(tok, shards)

    def one_image(image, start):
        end = start + lengths[0, image]
        low = start // tok
        count = jnp.maximum((end - 1) // tok - low + 1, least)
        first = jnp.minimum(low, shards - count)
        for size in range(least, most + 1):
            @pl.when(count == size)
            def _():
                work(image, size, first, start, end)
        return end

    lax.fori_loop(0, lengths.shape[1], one_image, jnp.int32(0))


def store_heads(ref, block, columns):
    heads, padded, _ = ref.shape
    filler = jnp.zeros((padded - HEAD_DIM, block.shape[1]), F32)
    for head in range(heads):
        rows = block[head * HEAD_DIM:(head + 1) * HEAD_DIM, :]
        ref[head, :, columns] = jnp.concatenate([rows, filler], axis=0).astype(BF16)


def joined(ref):
    return jnp.concatenate([ref[head, 0:HEAD_DIM, :] for head in range(ref.shape[0])], axis=0).astype(BF16)


def forward_kernel(early, len_ref, w_ref, in_ref, *refs):
    pieces = refs[:early]
    (q_s, k_s, vt_s, att_s, probs_s, d_s, wg_s, w_s, len_s, v_s, kt_s, sum_s, dy_s, len_sem, w_sem, dy_sem) = refs[early:]
    shards, height, tok = in_ref.shape
    part = height // 3
    heads = q_s.shape[0]
    scale = HEAD_DIM ** (-0.5)

    load_len = pltpu.make_async_copy(len_ref, len_s, len_sem)
    load_len.start()
    load_w = load_w_rows(w_ref, w_s, w_sem)
    loads = load_rows(pieces, dy_s, dy_sem)
    sum_s[...] = jnp.zeros_like(sum_s)
    for shard in range(shards):
        columns = slice(shard * tok, (shard + 1) * tok)
        for i, ref in enumerate((q_s, k_s, v_s)):
            store_heads(ref, in_ref[shard, i * part:(i + 1) * part, :].astype(F32), columns)
    for head in range(heads):
        kt_s[head] = k_s[head].T
        vt_s[head] = v_s[head].T
    load_len.wait()

    def work(image, count, first, start, end):
        width = count * tok
        base = pl.multiple_of(first * tok, tok)
        columns = pl.ds(base, width)
        key_pos = base + lax.broadcasted_iota(jnp.int32, (width, 1), 0)
        key_in = jnp.logical_and(key_pos >= start, key_pos < end)
        query_pos = base + lax.broadcasted_iota(jnp.int32, (1, width), 1)
        query_in = jnp.logical_and(query_pos >= start, query_pos < end)
        for head in range(heads):
            scores = jnp.where(key_in, dot(kt_s[head, columns, :], q_s[head, :, columns]), NEG_FILL)
            top = jnp.max(scores, axis=0, keepdims=True)
            grown = jnp.exp((scores - top) * scale)
            total = jnp.sum(grown, axis=0, keepdims=True)
            probs = (grown * jnp.where(query_in, 1.0 / total, 0.0)).astype(BF16)
            probs_s[image, head, 0:width, 0:width] = probs
            sum_s[head, :, columns] += dot(v_s[head, :, columns], probs)

    each_image(len_s, tok, shards, work)
    att_s[...] = joined(sum_s)
    for n in range(early, shards):
        dy_s[piece_columns(n, tok), :] = jnp.zeros((tok, dy_s.shape[1]), BF16)
    load_w.wait()
    for load in loads:
        load.wait()
    for shard in range(0, shards, 2):
        d_block = dot(w_s[...], dy_s[shard * tok:(shard + 2) * tok, :], NT)
        store_heads(d_s, d_block, slice(shard * tok, (shard + 2) * tok))
    wg_s[...] = dot(att_s[...], dy_s[...])


def backward_kernel(early, len_ref, w_s, q_s, k_s, vt_s, att_s, probs_s, d_ref, *refs):
    late = refs[:8 - early]
    outs = refs[8 - early:16 - early]
    (len_s, d_s, dq_s, dk_s, dv_s, out_s, len_sem, out_sem) = refs[16 - early:]
    shards, height, tok = out_s.shape
    part = height // 3
    heads = d_s.shape[0]
    scale = HEAD_DIM ** (-0.5)
    load_len = pltpu.make_async_copy(len_ref, len_s, len_sem)
    load_len.start()
    d_s[...] = d_ref[...]
    for ref in (dq_s, dk_s, dv_s):
        ref[...] = jnp.zeros_like(ref)
    for n, piece in enumerate(late):
        store_heads(d_s, dot(w_s[...], piece[...], NT), piece_columns(early + n, tok))
    load_len.wait()

    def work(image, count, first, start, end):
        width = count * tok
        columns = pl.ds(pl.multiple_of(first * tok, tok), width)
        att_all = att_s[:, columns].astype(F32)
        for head in range(heads):
            d = d_s[head, :, columns]
            probs = probs_s[image, head, 0:width, 0:width]
            att = att_all[head * HEAD_DIM:(head + 1) * HEAD_DIM, :]
            delta = jnp.sum(d.astype(F32)[0:HEAD_DIM, :] * att, axis=0, keepdims=True)
            d_probs = dot(vt_s[head, columns, :], d)
            d_scores = (scale * probs.astype(F32) * (d_probs - delta)).astype(BF16)
            dq_s[head, :, columns] += dot(k_s[head, :, columns], d_scores)
            dk_s[head, :, columns] += dot(q_s[head, :, columns], d_scores, NT)
            dv_s[head, :, columns] += dot(d, probs, NT)

    each_image(len_s, tok, shards, work)

    me = lax.axis_index("seq")
    stores = []
    for i, ref in enumerate((dq_s, dk_s, dv_s)):
        whole = joined(ref)
        rows = pl.ds(i * part, part)
        for shard in range(shards):
            out_s[shard, i * part:(i + 1) * part, :] = whole[:, shard * tok:(shard + 1) * tok]
        for n in BACK_ORDER[1:]:
            store = pltpu.make_async_copy(out_s.at[me ^ n, rows], outs[n].at[rows], out_sem.at[i, n])
            store.start()
            stores.append(store)
    outs[0][...] = out_s[me]
    for store in stores:
        store.wait()


def weight_kernel(early, att_ref, wg_ref, *refs):
    late, out_ref = refs[:-1], refs[-1]
    total = wg_ref[...]
    for n, piece in enumerate(late):
        total = total + dot(att_ref[:, piece_columns(early + n, piece.shape[0])], piece[...])
    out_ref[...] = total.astype(BF16)


def load_w_rows(w_ref, w_s, sem):
    part = w_s.shape[0]
    row = pl.multiple_of(lax.axis_index("seq") * part, part)
    load = pltpu.make_async_copy(w_ref.at[pl.ds(row, part), :], w_s, sem)
    load.start()
    return load


def piece_columns(n, tok):
    me = lax.axis_index("seq")
    owner = me ^ jnp.where(is_inner(me), INNER_SOURCES[n], OUTER_SOURCES[n])
    return pl.ds(pl.multiple_of(owner * tok, tok), tok)


def load_rows(pieces, dy_s, sems):
    loads = []
    for n, piece in enumerate(pieces):
        load = pltpu.make_async_copy(piece, dy_s.at[piece_columns(n, piece.shape[0]), :], sems.at[n])
        load.start()
        loads.append(load)
    return loads


BACK_ORDER = (0, 5, 3, 4, 7, 6, 2, 1)
FIFTH_PARTS = 4
INNER_SOURCES = (0, 2, 6, 4, 3, 1, 7, 5)
OUTER_SOURCES = (0, 2, 1, 3, 4, 6, 5, 7)


def is_inner(index):
    z = index // 2
    return jnp.logical_or(z == 1, z == 2)


def gather_steps(block, event):
    devices = range(8)
    along = [(i, i ^ 2) for i in devices]
    across = [(i, i ^ 1) for i in devices]
    middle = [(i, i ^ 6 if i // 2 in (1, 2) else i ^ 1) for i in devices]
    inner = is_inner(lax.axis_index("seq"))

    def move(value, pairs):
        return lax.ppermute(value, "seq", pairs)

    one = move(block, along)
    two = move(block, middle)
    one, two = after(one, event), after(two, event)
    three = move(one, middle)
    four = move(two, along)
    rows = block.shape[0] // FIFTH_PARTS
    five = jnp.concatenate([move(three[n * rows:(n + 1) * rows], along) for n in range(FIFTH_PARTS)])
    six = move(jnp.where(inner, two, four), across)
    seven = move(jnp.where(inner, three, five), across)
    return (block, one, two, three, four, five, six, seven)


def after(value, *events):
    return lax.optimization_barrier((value, *events))[0]


def in_hbm(*arrays):
    return [pltpu.with_memory_space_constraint(array, pltpu.HBM) for array in arrays]


def head_body(queries, keys, values, out_weight, out_grad, lengths):
    tok, width = queries.shape[1:]
    shards = lax.axis_size("seq")
    groups = lax.axis_size("dp")
    part = width // shards
    heads = HEADS // shards
    tokens = tok * shards
    padded = -(-HEAD_DIM // 16) * 16

    def shape(dims, kind=BF16):
        return jax.ShapeDtypeStruct(dims, kind)

    sent = pl.pallas_call(
        spread_kernel, out_shape=pltpu.HBM((shards, 3 * part, tok), BF16),
        in_specs=[HBM] * 3, out_specs=HBM, compiler_params=PARAMS,
        scratch_shapes=[pltpu.VMEM((3, tok, width), BF16), pltpu.VMEM((3, shards, part, tok), BF16), DMA((3,)), DMA((3,))],
    )(*in_hbm(queries[0], keys[0], values[0]))
    pieces = gather_steps(out_grad[0], sent)
    arrived = lax.all_to_all(after(sent, *pieces[1:3]), "seq", 0, 0, tiled=True)

    images = lengths.shape[1]
    window = window_sizes(tok, shards)[1] * tok
    wide, tall = (heads, padded, tokens), (heads, tokens, padded)
    flat, chance = (part, tokens), (images, heads, window, window)

    def scratch(*dims, kind=BF16):
        return [pltpu.VMEM(d, kind) for d in dims]

    len_s = pltpu.SMEM((1, images), jnp.int32)
    early = 6
    late = len(pieces) - early
    q_t, k_t, v_r, attended, probs, d_part, w_early, w_rows = pl.pallas_call(
        functools.partial(forward_kernel, early),
        out_shape=[shape(wide), shape(wide), shape(tall), shape(flat), shape(chance), shape(wide), shape((part, width), F32), shape((part, width))],
        in_specs=[HBM, HBM, VMEM] + [HBM] * early, out_specs=[VMEM] * 8, compiler_params=PARAMS,
        scratch_shapes=[len_s] + scratch(wide, tall) + scratch(wide, kind=F32) + scratch((tokens, width))
        + [DMA, DMA, DMA((early,))],
    )(*in_hbm(lengths, out_weight), arrived, *in_hbm(*pieces[:early]))
    w_part = pl.pallas_call(
        functools.partial(weight_kernel, early), out_shape=shape((part, width)),
        in_specs=[VMEM] * (2 + late), out_specs=VMEM, compiler_params=PARAMS,
    )(attended, w_early, *pieces[early:])
    grads = pl.pallas_call(
        functools.partial(backward_kernel, early),
        out_shape=[shape((3 * part, tok))] + [pltpu.HBM((3 * part, tok), BF16)] * (shards - 1),
        in_specs=[HBM] + [VMEM] * (7 + late), out_specs=[VMEM] + [HBM] * (shards - 1), compiler_params=PARAMS,
        scratch_shapes=[len_s] + scratch(wide) + scratch(wide, wide, wide, kind=F32)
        + scratch((shards, 3 * part, tok)) + [DMA, DMA((3, shards))],
    )(*in_hbm(lengths), w_rows, q_t, k_t, v_r, attended, probs, d_part, *pieces[early:])
    sums = w_part.astype(F32)
    step = 1
    while step < groups:
        pairs = [(i, i ^ step) for i in range(groups)]
        sums = w_part.astype(F32) + lax.ppermute(w_part, "dp", pairs).astype(F32)
        w_part = lax.reduce_precision(sums, 8, 7).astype(BF16)
        step *= 2
    weight_grad = sums * (1.0 / math.sqrt(tokens * groups))

    returned = [grads[0]]
    for n in BACK_ORDER[1:]:
        block = after(grads[n], weight_grad) if n == BACK_ORDER[-1] else grads[n]
        returned.append(lax.ppermute(block, "seq", [(i, i ^ n) for i in range(shards)]))

    q_grad, k_grad, v_grad = pl.pallas_call(
        collect_kernel, out_shape=[shape((tok, width), F32)] * 3, in_specs=[VMEM] * shards, out_specs=[ANY] * 3,
        compiler_params=PARAMS,
        scratch_shapes=scratch((shards, 3 * part, tok)) + scratch((3, tok, width), kind=F32) + [DMA((3,))],
    )(*returned)
    return q_grad[None], k_grad[None], v_grad[None], weight_grad


def solution(mesh):
    in_specs = (
        P("dp", "seq", None),
        P("dp", "seq", None),
        P("dp", "seq", None),
        P(),
        P("dp", "seq", None),
        P("dp", None),
    )
    out_specs = (P("dp", "seq", None), P("dp", "seq", None), P("dp", "seq", None), P("seq", None))
    by_heads = mesh.shape["seq"] == 8 and mesh.shape["dp"] & (mesh.shape["dp"] - 1) == 0
    body = head_body if by_heads else halo_body
    return jax.shard_map(body, mesh=mesh, in_specs=in_specs, out_specs=out_specs, check_vma=False)
```
